32 devices in a mesh: row: 4 (over z), col: 4 (over y, core), layer: 2 (over x).
Axes of the slice: x: 2, y: 2, z: 4, core: 2. Of those that a mesh axis runs over, the one named last changes fastest.
Arguments:
- density: bfloat16 [16, 13, 256, 256], P(('row', 'col')), as said below
- pattern: int32 [16, 13], P(('row', 'col')), may hold values from 0 to 1, as said below
Outputs:
- purified: float32 [16, 13, 256, 256], P(('row', 'col'), None, None, 'layer')
The draws below stay inside these ranges and needn't reach their ends.
Inputs may be any that keep to these rules, and one draw needn't show every extreme that they name: pattern[i, 6 + d] = pattern[i + d mod 16, 6 - d], and pattern[i, 6] = 1. density[i, 6 + d] is the transpose of density[i + d mod 16, 6 - d], and it is zero where pattern is 0.
All inputs are finite; a program needn't handle non-finite values.
Results may differ from the reference program's by a relative error of at most 0.0039.
The reference program's roundings to bfloat16 on the way (of `square_half`) count: a program that leaves them out, or rounds other values in their place, can miss the bound.
Values may be sent and summed in bfloat16 or wider, within the bound.
No kernel may reach another device: no remote copies, remote signals or barrier semaphores. Data moves between devices by JAX's collectives and lax.ppermute only.
A program may use at most 64 MiB of HBM per device.

```python
from functools import reduce
import jax
import jax.numpy as jnp
from jax import lax

BLOCK = 256
HALF = 6
NB = 16


def kept_bands(key):
    upper = (jax.random.randint(jax.random.fold_in(key, 5), (NB, HALF), 0, 4) != 0).astype(jnp.int32)
    columns = []
    for offset in range(-HALF, HALF + 1):
        if offset == 0:
            columns.append(jnp.ones((NB,), jnp.int32))
        elif offset > 0:
            columns.append(upper[:, offset - 1])
        else:
            columns.append(jnp.roll(upper[:, -offset - 1], -offset))
    return jnp.stack(columns, axis=1)


def draw_pattern(key, part):
    return kept_bands(key)


def draw_density(key, part):
    kept = kept_bands(key).astype(jnp.float32)
    first_key = jax.random.fold_in(key, 11)
    raw = jax.random.normal(first_key, (NB, 2 * HALF + 1, BLOCK, BLOCK), jnp.float32)
    scales = jnp.ones((NB, BLOCK), jnp.float32)
    pieces = []
    for offset in range(-HALF, HALF + 1):
        mirror = jnp.roll(raw[:, HALF - offset], -offset, axis=0)
        blocks = (raw[:, HALF + offset] + jnp.swapaxes(mirror, 1, 2)) * 0.7071
        blocks = blocks * jnp.roll(scales, -offset, axis=0)[:, None, :]
        if offset == 0:
            blocks = blocks * 0.01 + 0.5 * jnp.eye(BLOCK, dtype=jnp.float32)[None]
        else:
            blocks = blocks * 0.01
        pieces.append(blocks)
    value = jnp.stack(pieces, axis=1) * kept[:, :, None, None]
    return value.astype(jnp.bfloat16)


def setup_inputs(seed: int = 0) -> dict:
    seeds = jax.random.split(jax.random.key(seed), 3)
    return {
        "density": draw_density(jax.random.fold_in(seeds[2], 71), 0),
        "pattern": draw_pattern(jax.random.fold_in(seeds[2], 71), 0),
    }


def band_product(factor, right, half):
    band = 2 * half + 1
    collected = [[] for position in range(band)]
    for offset in range(-half, half + 1):
        right_rows = jnp.roll(right, -offset, axis=0)
        if offset >= 0:
            first = offset
            source = right_rows[:, :band - offset]
        else:
            first = 0
            source = right_rows[:, -offset:]
        product = jnp.einsum("rab,rdbc->rdac", factor[:, half + offset], source, precision=lax.Precision.HIGHEST)
        for column in range(product.shape[1]):
            collected[first + column].append(product[:, column])
    return jnp.stack([reduce(lambda first_item, second_item: first_item + second_item, items) for items in collected], axis=1)


def reference(density, pattern):
    keep = pattern.astype(jnp.float32)[:, :, None, None]
    dense = density.astype(jnp.float32)
    square = band_product(dense, dense, HALF) * keep
    square_half = lax.optimization_barrier(square.astype(jnp.bfloat16))
    cube = band_product(square_half.astype(jnp.float32), dense, HALF) * keep
    return 3.0 * square - 2.0 * cube
```

```python
import jax
import jax.numpy as jnp
from jax import lax
from jax.experimental import pallas as pl
from jax.experimental.pallas import tpu as pltpu
from jax.sharding import PartitionSpec as P

HALF = 6
BAND = 2 * HALF + 1
FORWARD = ((0, 1, 2, 3, 4, 5, -3, -5), (0, 1, 2, 3), (0, 1))
BACKWARD = ((0, 1, 2, 3, 4, -4, -5, -6), (0, 1, 2, -6), (0, 0))
SIZES = tuple(len(part) for part in FORWARD)
FETCHED = sum(SIZES)
LANES = 128
FRAME = range(-HALF, HALF + 1)


def places():
    held = {}
    for offset in FRAME:
        held[0, offset] = offset + HALF
    for offset in FRAME:
        held.setdefault((1, 1 + offset), BAND + offset + HALF)
    slot = 2 * BAND
    for other in (False, True):
        for parts, way in ((FORWARD, 1), (BACKWARD, -1)):
            for step, part in enumerate(parts):
                for offset in part:
                    row = way * 2 * (step + 1)
                    column = row + way * offset
                    if other:
                        row, column = 1 - row, 1 - column
                    if (row, column) not in held and (column, row) not in held:
                        held[row, column] = slot
                    slot += 1
    return held


HELD = places()


def terms(column):
    plain = []
    turned = []
    for row in FRAME:
        if abs(row - column) <= HALF:
            if (row, column) in HELD:
                plain.append((row, HELD[row, column]))
            else:
                turned.append((row, HELD[column, row]))
    return plain, turned


def column_product(left, plain_block, turned_block, column):
    plain, turned = terms(column)
    total = None
    if plain:
        total = jnp.dot(
            jnp.concatenate([left(row) for row, slot in plain], axis=1),
            jnp.concatenate([plain_block(slot) for row, slot in plain], axis=0),
            preferred_element_type=jnp.float32,
        )
    if turned:
        other = lax.dot_general(
            jnp.concatenate([left(row) for row, slot in turned], axis=1),
            jnp.concatenate([turned_block(slot) for row, slot in turned], axis=1),
            (((1,), (1,)), ((), ())),
            preferred_element_type=jnp.float32,
        )
        total = other if total is None else total + other
    return total


def pack_kernel(index, density, first, second, third, sems):
    copies = []
    place = 0
    for out in (first, second, third):
        for item in range(out.shape[1]):
            copies.append(
                pltpu.make_async_copy(
                    density.at[0, index[place]], out.at[0, item], sems.at[place]
                )
            )
            place += 1
    for copy in copies:
        copy.start()
    for copy in copies:
        copy.wait()


def pack(density, index):
    block = density.shape[2]
    return pl.pallas_call(
        pack_kernel,
        out_shape=[
            jax.ShapeDtypeStruct((1, size, block, block), density.dtype) for size in SIZES
        ],
        in_specs=[
            pl.BlockSpec(memory_space=pltpu.SMEM),
            pl.BlockSpec(memory_space=pl.ANY),
        ],
        out_specs=[pl.BlockSpec(memory_space=pl.ANY)] * len(SIZES),
        scratch_shapes=[pltpu.SemaphoreType.DMA((FETCHED,))],
        name="pack",
    )(index, density)


def purify_kernel(where, keep, own, beside, *refs):
    sources, (out, slots, rounded, square, result, in_sems, out_sems) = refs[:12], refs[12:]
    way = where[0]
    kind = where[1]
    part = where[2]
    copies = []

    def bring(source, target):
        copies.append(pltpu.make_async_copy(source, target, in_sems.at[len(copies)]))

    for offset in FRAME:
        bring(own.at[0, HALF + way * offset], slots.at[offset + HALF])
        bring(beside.at[0, HALF + way * offset], slots.at[BAND + offset + HALF])
    for group in range(2):
        base = 2 * BAND + group * 2 * FETCHED
        start = 0
        for step, size in enumerate(SIZES):
            near = sources[group * 6 + step]
            far = sources[group * 6 + 3 + step]
            bring(near.at[0], slots.at[pl.ds(base + kind * FETCHED + start, size)])
            bring(far.at[0], slots.at[pl.ds(base + (1 - kind) * FETCHED + start, size)])
            start += size
    for copy in copies:
        copy.start()
    for copy in copies:
        copy.wait()

    lanes = pl.ds(pl.multiple_of(part * LANES, LANES), LANES)
    for column in FRAME:
        total = column_product(
            lambda row: slots[row + HALF], lambda slot: slots[slot], lambda slot: slots[slot], column
        )
        total = total * keep[0, HALF + way * column].astype(jnp.float32)
        rounded[column + HALF] = total.astype(jnp.bfloat16)
        mine = total[:, :LANES]
        for piece in range(1, total.shape[1] // LANES):
            mine = jnp.where(part == piece, total[:, piece * LANES : (piece + 1) * LANES], mine)
        square[column + HALF] = mine
    written = []
    for column in FRAME:
        total = column_product(
            lambda row: rounded[row + HALF],
            lambda slot: slots[slot, :, lanes],
            lambda slot: slots[slot, lanes, :],
            column,
        )
        total = total * keep[0, HALF + way * column].astype(jnp.float32)
        result[column + HALF] = 3.0 * square[column + HALF] - 2.0 * total
        copy = pltpu.make_async_copy(
            result.at[column + HALF], out.at[0, HALF + way * column], out_sems.at[column + HALF]
        )
        copy.start()
        written.append(copy)
    for copy in written:
        copy.wait()


def purify(where, keep, own, beside, fetched):
    block = own.shape[2]
    copies = 2 * BAND + len(fetched)
    return pl.pallas_call(
        purify_kernel,
        out_shape=jax.ShapeDtypeStruct((1, BAND, block, LANES), jnp.float32),
        in_specs=[pl.BlockSpec(memory_space=pltpu.SMEM)] * 2
        + [pl.BlockSpec(memory_space=pl.ANY)] * (2 + len(fetched)),
        out_specs=pl.BlockSpec(memory_space=pl.ANY),
        scratch_shapes=[
            pltpu.VMEM((2 * BAND + 4 * FETCHED, block, block), jnp.bfloat16),
            pltpu.VMEM((BAND, block, block), jnp.bfloat16),
            pltpu.VMEM((BAND, block, LANES), jnp.float32),
            pltpu.VMEM((BAND, block, LANES), jnp.float32),
            pltpu.SemaphoreType.DMA((copies,)),
            pltpu.SemaphoreType.DMA((BAND,)),
        ],
        compiler_params=pltpu.CompilerParams(vmem_limit_bytes=48 * 2**20),
        cost_estimate=pl.CostEstimate(
            flops=6 * 127 * block**3, bytes_accessed=14 * 2**20, transcendentals=0
        ),
        name="purify",
    )(where, keep, own, beside, *fetched)


def body(density, pattern):
    axes = ("row", "col", "layer")
    rows = lax.axis_size(("row", "col"))
    layers = lax.axis_size("layer")
    width = density.shape[2] // layers
    row = lax.axis_index(("row", "col"))
    layer = lax.axis_index("layer")
    way = 1 - 2 * (row % 2)
    kind = layer % 2

    def fetch(array, step):
        pairs = []
        for source in range(rows):
            for plane in range(layers):
                shift = 2 * step * (1 - 2 * (source % 2)) * (1 - 2 * (plane % 2))
                pairs.append((source * layers + plane, (source - shift) % rows * layers + plane))
        return lax.ppermute(array, axes, pairs)

    def swap_layers(array):
        return lax.ppermute(array, "layer", [(plane, plane ^ 1) for plane in range(layers)])

    def swap_cores(array):
        peers = lax.axis_size("col")
        return lax.ppermute(array, "col", [(peer, peer ^ 1) for peer in range(peers)])

    lists = jnp.where(
        kind == 0,
        jnp.array([offset for part in FORWARD for offset in part], jnp.int32),
        -jnp.array([offset for part in BACKWARD for offset in part], jnp.int32),
    )
    parts = pack(density, HALF + way * lists)
    beside = swap_cores(density)
    near = [fetch(part, step + 1) for step, part in enumerate(parts)]
    far = [swap_layers(part) for part in near]
    fetched = near + far + [swap_cores(part) for part in near + far]
    where = jnp.stack([way, kind, layer * width // LANES]).astype(jnp.int32)
    out = purify(where, pattern, density, beside, fetched)
    if width < LANES:
        out = lax.dynamic_slice_in_dim(out, layer * width % LANES, width, 3)
    return out


def solution(mesh):
    return jax.shard_map(
        body,
        mesh=mesh,
        in_specs=(P(("row", "col"), None, None, None), P(("row", "col"), None)),
        out_specs=P(("row", "col"), None, None, "layer"),
        check_vma=False,
    )
```

```python
import jax
import jax.numpy as jnp
from jax import lax
from jax.experimental import pallas as pl
from jax.experimental.pallas import tpu as pltpu
from jax.sharding import PartitionSpec as P

HALF = 6
BAND = 2 * HALF + 1
FORWARD = ((0, 1, 2, 3, 4, 5, -3, -5), (0, 1, 2, 3), (0, 1))
BACKWARD = ((0, 1, 2, 3, 4, -4, -5, -6), (0, 1, 2, -6), (0, 0))
SIZES = tuple(len(part) for part in FORWARD)
FETCHED = sum(SIZES)
LANES = 128
FRAME = range(-HALF, HALF + 1)


def places():
    held = {}
    for offset in FRAME:
        held[0, offset] = offset + HALF
    for offset in FRAME:
        held.setdefault((1, 1 + offset), BAND + offset + HALF)
    slot = 2 * BAND
    for other in (False, True):
        for parts, way in ((FORWARD, 1), (BACKWARD, -1)):
            for step, part in enumerate(parts):
                for offset in part:
                    row = way * 2 * (step + 1)
                    column = row + way * offset
                    if other:
                        row, column = 1 - row, 1 - column
                    if (row, column) not in held and (column, row) not in held:
                        held[row, column] = slot
                    slot += 1
    return held


HELD = places()


def terms(column):
    plain = []
    turned = []
    for row in FRAME:
        if abs(row - column) <= HALF:
            if (row, column) in HELD:
                plain.append((row, HELD[row, column]))
            else:
                turned.append((row, HELD[column, row]))
    return plain, turned


def column_product(left, plain_block, turned_block, column):
    plain, turned = terms(column)
    total = None
    if plain:
        total = jnp.dot(
            jnp.concatenate([left(row) for row, slot in plain], axis=1),
            jnp.concatenate([plain_block(slot) for row, slot in plain], axis=0),
            preferred_element_type=jnp.float32,
        )
    if turned:
        other = lax.dot_general(
            jnp.concatenate([left(row) for row, slot in turned], axis=1),
            jnp.concatenate([turned_block(slot) for row, slot in turned], axis=1),
            (((1,), (1,)), ((), ())),
            preferred_element_type=jnp.float32,
        )
        total = other if total is None else total + other
    return total


def pack_kernel(index, density, first, second, third, sems):
    copies = []
    place = 0
    for out in (first, second, third):
        for item in range(out.shape[1]):
            copies.append(
                pltpu.make_async_copy(
                    density.at[0, index[place]], out.at[0, item], sems.at[place]
                )
            )
            place += 1
    for copy in copies:
        copy.start()
    for copy in copies:
        copy.wait()


def pack(density, index):
    block = density.shape[2]
    return pl.pallas_call(
        pack_kernel,
        out_shape=[
            jax.ShapeDtypeStruct((1, size, block, block), density.dtype) for size in SIZES
        ],
        in_specs=[
            pl.BlockSpec(memory_space=pltpu.SMEM),
            pl.BlockSpec(memory_space=pl.ANY),
        ],
        out_specs=[pl.BlockSpec(memory_space=pltpu.VMEM)] * len(SIZES),
        scratch_shapes=[pltpu.SemaphoreType.DMA((FETCHED,))],
        name="pack",
    )(index, density)


def purify_kernel(where, keep, own, beside, *refs):
    sources, (out, slots, rounded, square, result, in_sems, out_sems) = refs[:12], refs[12:]
    way = where[0]
    kind = where[1]
    part = where[2]
    copies = []

    def bring(source, target):
        copies.append(pltpu.make_async_copy(source, target, in_sems.at[len(copies)]))

    for offset in FRAME:
        bring(own.at[0, HALF + way * offset], slots.at[offset + HALF])
        bring(beside.at[0, HALF + way * offset], slots.at[BAND + offset + HALF])
    for group in range(2):
        base = 2 * BAND + group * 2 * FETCHED
        start = 0
        for step, size in enumerate(SIZES):
            near = sources[group * 6 + step]
            far = sources[group * 6 + 3 + step]
            bring(near.at[0], slots.at[pl.ds(base + kind * FETCHED + start, size)])
            bring(far.at[0], slots.at[pl.ds(base + (1 - kind) * FETCHED + start, size)])
            start += size
    for copy in copies:
        copy.start()
    for copy in copies:
        copy.wait()

    lanes = pl.ds(pl.multiple_of(part * LANES, LANES), LANES)
    for column in FRAME:
        total = column_product(
            lambda row: slots[row + HALF], lambda slot: slots[slot], lambda slot: slots[slot], column
        )
        total = total * keep[0, HALF + way * column].astype(jnp.float32)
        rounded[column + HALF] = total.astype(jnp.bfloat16)
        mine = total[:, :LANES]
        for piece in range(1, total.shape[1] // LANES):
            mine = jnp.where(part == piece, total[:, piece * LANES : (piece + 1) * LANES], mine)
        square[column + HALF] = mine
    written = []
    for column in FRAME:
        total = column_product(
            lambda row: rounded[row + HALF],
            lambda slot: slots[slot, :, lanes],
            lambda slot: slots[slot, lanes, :],
            column,
        )
        total = total * keep[0, HALF + way * column].astype(jnp.float32)
        result[column + HALF] = 3.0 * square[column + HALF] - 2.0 * total
        copy = pltpu.make_async_copy(
            result.at[column + HALF], out.at[0, HALF + way * column], out_sems.at[column + HALF]
        )
        copy.start()
        written.append(copy)
    for copy in written:
        copy.wait()


def purify(where, keep, own, beside, fetched):
    block = own.shape[2]
    copies = 2 * BAND + len(fetched)
    return pl.pallas_call(
        purify_kernel,
        out_shape=jax.ShapeDtypeStruct((1, BAND, block, LANES), jnp.float32),
        in_specs=[pl.BlockSpec(memory_space=pltpu.SMEM)] * 2
        + [pl.BlockSpec(memory_space=pl.ANY)] * (2 + len(fetched)),
        out_specs=pl.BlockSpec(memory_space=pl.ANY),
        scratch_shapes=[
            pltpu.VMEM((2 * BAND + 4 * FETCHED, block, block), jnp.bfloat16),
            pltpu.VMEM((BAND, block, block), jnp.bfloat16),
            pltpu.VMEM((BAND, block, LANES), jnp.float32),
            pltpu.VMEM((BAND, block, LANES), jnp.float32),
            pltpu.SemaphoreType.DMA((copies,)),
            pltpu.SemaphoreType.DMA((BAND,)),
        ],
        compiler_params=pltpu.CompilerParams(vmem_limit_bytes=48 * 2**20),
        cost_estimate=pl.CostEstimate(
            flops=6 * 127 * block**3, bytes_accessed=14 * 2**20, transcendentals=0
        ),
        name="purify",
    )(where, keep, own, beside, *fetched)


def body(density, pattern):
    axes = ("row", "col", "layer")
    rows = lax.axis_size(("row", "col"))
    layers = lax.axis_size("layer")
    width = density.shape[2] // layers
    row = lax.axis_index(("row", "col"))
    layer = lax.axis_index("layer")
    way = 1 - 2 * (row % 2)
    kind = layer % 2

    def fetch(array, step):
        pairs = []
        for source in range(rows):
            for plane in range(layers):
                shift = 2 * step * (1 - 2 * (source % 2)) * (1 - 2 * (plane % 2))
                pairs.append((source * layers + plane, (source - shift) % rows * layers + plane))
        return lax.ppermute(array, axes, pairs)

    def swap_layers(array):
        return lax.ppermute(array, "layer", [(plane, plane ^ 1) for plane in range(layers)])

    def swap_cores(array):
        peers = lax.axis_size("col")
        return lax.ppermute(array, "col", [(peer, peer ^ 1) for peer in range(peers)])

    lists = jnp.where(
        kind == 0,
        jnp.array([offset for part in FORWARD for offset in part], jnp.int32),
        -jnp.array([offset for part in BACKWARD for offset in part], jnp.int32),
    )
    parts = pack(density, HALF + way * lists)
    beside = swap_cores(density)
    near = [fetch(part, step + 1) for step, part in enumerate(parts)]
    far = [swap_layers(part) for part in near]
    fetched = near + far + [swap_cores(part) for part in near + far]
    where = jnp.stack([way, kind, layer * width // LANES]).astype(jnp.int32)
    out = purify(where, pattern, density, beside, fetched)
    if width < LANES:
        out = lax.dynamic_slice_in_dim(out, layer * width % LANES, width, 3)
    return out


def solution(mesh):
    return jax.shard_map(
        body,
        mesh=mesh,
        in_specs=(P(("row", "col"), None, None, None), P(("row", "col"), None)),
        out_specs=P(("row", "col"), None, None, "layer"),
        check_vma=False,
    )
```

```python
import jax
import jax.numpy as jnp
from jax import lax
from jax.experimental import pallas as pl
from jax.experimental.pallas import tpu as pltpu
from jax.sharding import PartitionSpec as P

HALF = 6
BAND = 2 * HALF + 1
FORWARD = ((0, 1, 2, 3, 4, 5, -3, -5), (0, 1, 2, 3), (0, 1))
BACKWARD = ((0, 1, 2, 3, 4, -4, -5, -6), (0, 1, 2, -6), (0, 0))
SIZES = tuple(len(part) for part in FORWARD)
WHOLE, MIDDLE, OUTER = SIZES
PART = WHOLE // 2
STARTS = (0, WHOLE, WHOLE + MIDDLE)
FETCHED = sum(SIZES)
LANES = 128
FRAME = range(-HALF, HALF + 1)


def places():
    held = {}
    for offset in FRAME:
        held[0, offset] = offset + HALF
    for offset in FRAME:
        held.setdefault((1, 1 + offset), BAND + offset + HALF)
    slot = 2 * BAND
    for other in (False, True):
        for parts, way in ((FORWARD, 1), (BACKWARD, -1)):
            for step, part in enumerate(parts):
                for offset in part:
                    row = way * 2 * (step + 1)
                    column = row + way * offset
                    if other:
                        row, column = 1 - row, 1 - column
                    if (row, column) not in held and (column, row) not in held:
                        held[row, column] = slot
                    slot += 1
    return held


HELD = places()
def stage(slot):
    if slot < 2 * BAND:
        return 0
    return 1 if (slot - 2 * BAND) % FETCHED >= WHOLE else 2


def terms(column, stages=(0, 1, 2)):
    plain = {}
    turned = {}
    for row in FRAME:
        if abs(row - column) <= HALF:
            if (row, column) in HELD:
                slot, group = HELD[row, column], plain
            else:
                slot, group = HELD[column, row], turned
            if stage(slot) in stages:
                group[row] = slot
    return plain, turned


def pairs():
    def shared(one, two):
        return sum(len(first.keys() & other.keys()) for first, other in zip(terms(one), terms(two)))

    def best(left):
        if len(left) < 2:
            return 0, [left] if left else []
        choices = []
        for place in range(1, len(left)):
            count, rest = best(left[1:place] + left[place + 1 :])
            choices.append((count + shared(left[0], left[place]), [(left[0], left[place])] + rest))
        if len(left) % 2:
            count, rest = best(left[1:])
            choices.append((count, [(left[0],)] + rest))
        return max(choices, key=lambda choice: choice[0])

    return best(tuple(FRAME))[1]


PAIRS = pairs()


def product(lefts, blocks, turned):
    return lax.dot_general(
        jnp.concatenate(lefts, axis=1),
        jnp.concatenate(blocks, axis=1 if turned else 0),
        (((1,), (1 if turned else 0,)), ((), ())),
        preferred_element_type=jnp.float32,
    )


def column_product(left, block, column, stages):
    total = None
    for turned, group in enumerate(terms(column, stages)):
        if group:
            part = product(
                [left(row) for row in group], [block(slot) for slot in group.values()], turned
            )
            total = part if total is None else total + part
    return total


def part_products(left, part, columns):
    totals = [None] * len(columns)

    def add(place, value):
        totals[place] = value if totals[place] is None else totals[place] + value

    for turned in (0, 1):
        groups = [terms(column)[turned] for column in columns]
        both = [row for row in groups[0] if all(row in group for group in groups)]
        if len(columns) > 1 and both:
            blocks = [
                jnp.concatenate([part(group[row], turned) for group in groups], axis=0 if turned else 1)
                for row in both
            ]
            value = product([left(row) for row in both], blocks, turned)
            for place in range(len(columns)):
                add(place, value[:, place * LANES : (place + 1) * LANES])
        for place, group in enumerate(groups):
            alone = [row for row in group if len(columns) == 1 or row not in both]
            if alone:
                blocks = [part(group[row], turned) for row in alone]
                add(place, product([left(row) for row in alone], blocks, turned))
    return totals


def position():
    row = lax.axis_index(("row", "col"))
    return 1 - 2 * (row % 2), lax.axis_index("layer") % 2, (row + row // 2) % 2


def pack_kernel(density, diag, middle, outer, pure):
    way, layer_kind, row_kind = position()

    def bring(out, item, forward, backward, backwards):
        index = HALF + way * jnp.where(backwards == 0, forward, -backward)
        out[0, item] = density[0, index]

    for item in range(PART):
        forward = jnp.where(layer_kind == 0, FORWARD[0][item], FORWARD[0][PART + item])
        backward = jnp.where(layer_kind == 0, BACKWARD[0][item], BACKWARD[0][PART + item])
        bring(diag, item, forward, backward, row_kind)
    for out, step in ((middle, 1), (outer, 2)):
        for item in range(SIZES[step]):
            bring(out, item, FORWARD[step][item], BACKWARD[step][item], layer_kind)
    for item in range(WHOLE):
        bring(pure, item, FORWARD[0][item], BACKWARD[0][item], 1 - row_kind)


def frame_row(way, array):
    return lambda offset: array[0, HALF + way * offset]


def first_kernel(own, beside, sums):
    way, layer_kind, row_kind = position()
    left = frame_row(way, own)
    right = frame_row(way, beside)
    for column in FRAME:
        block = lambda slot: left(slot - HALF) if slot < BAND else right(slot - BAND - HALF)
        sums[column + HALF] = column_product(left, block, column, (0,))


def second_kernel(own, *refs):
    sources, (before, sums, far, sems) = refs[:8], refs[8:]
    way, layer_kind, row_kind = position()
    copies = []
    for group in range(2):
        for step, start in ((1, 0), (2, MIDDLE)):
            for place in range(2):
                source = sources[group * 4 + (step - 1) * 2 + place]
                kind = layer_kind if place == 0 else 1 - layer_kind
                base = (group * 2 + kind) * (MIDDLE + OUTER) + start
                copies.append(
                    pltpu.make_async_copy(
                        source.at[0], far.at[pl.ds(base, SIZES[step])], sems.at[len(copies)]
                    )
                )
    for copy in copies:
        copy.start()
    for copy in copies:
        copy.wait()
    left = frame_row(way, own)
    for column in FRAME:
        block = lambda slot: far[far_place(slot)]
        total = column_product(left, block, column, (1,))
        sums[column + HALF] = before[column + HALF] + (0.0 if total is None else total)


def far_place(slot):
    group, item = divmod(slot - 2 * BAND, FETCHED)
    return group * (MIDDLE + OUTER) + item - WHOLE


def last_kernel(keep, own, beside, far, *refs):
    sources, refs = refs[:6], refs[6:]
    before, out, following, rounded, square, result, sems, out_sems = refs
    way, layer_kind, row_kind = position()
    part = lax.axis_index("layer") * (own.shape[2] // lax.axis_size("layer")) // LANES
    copies = []

    def bring(source, first, size):
        copies.append(
            pltpu.make_async_copy(
                source.at[0], following.at[pl.ds(first, size)], sems.at[len(copies)]
            )
        )

    for group in range(2):
        pure, near, remote = sources[group * 3 : group * 3 + 3]
        kind = row_kind if group == 0 else 1 - row_kind
        bring(pure, (group * 2 + kind) * WHOLE, WHOLE)
        base = (group * 2 + 1 - kind) * WHOLE
        bring(near, base + layer_kind * PART, PART)
        bring(remote, base + (1 - layer_kind) * PART, PART)
    for copy in copies:
        copy.start()
    for copy in copies:
        copy.wait()

    left = frame_row(way, own)

    def next_place(slot):
        group, item = divmod(slot - 2 * BAND, FETCHED)
        return group * WHOLE + item

    for column in FRAME:
        total = column_product(left, lambda slot: following[next_place(slot)], column, (2,))
        total = before[column + HALF] + (0.0 if total is None else total)
        total = total * keep[0, HALF + way * column].astype(jnp.float32)
        rounded[column + HALF] = total.astype(jnp.bfloat16)
        mine = total[:, :LANES]
        for piece in range(1, total.shape[1] // LANES):
            mine = jnp.where(part == piece, total[:, piece * LANES : (piece + 1) * LANES], mine)
        square[column + HALF] = mine

    lanes = pl.ds(pl.multiple_of(part * LANES, LANES), LANES)

    def piece(slot, turned):
        if slot < BAND:
            array, index = own, (0, HALF + way * (slot - HALF))
        elif slot < 2 * BAND:
            array, index = beside, (0, HALF + way * (slot - BAND - HALF))
        elif stage(slot) == 1:
            array, index = far, (far_place(slot),)
        else:
            array, index = following, (next_place(slot),)
        return array[(*index, lanes, slice(None)) if turned else (*index, slice(None), lanes)]

    written = []
    for columns in PAIRS:
        totals = part_products(lambda row: rounded[row + HALF], piece, columns)
        for column, total in zip(columns, totals):
            total = total * keep[0, HALF + way * column].astype(jnp.float32)
            result[column + HALF] = 3.0 * square[column + HALF] - 2.0 * total
            copy = pltpu.make_async_copy(
                result.at[column + HALF], out.at[0, HALF + way * column], out_sems.at[column + HALF]
            )
            copy.start()
            written.append(copy)
    for copy in written:
        copy.wait()


SCALARS = pl.BlockSpec(memory_space=pltpu.SMEM)
ANYWHERE = pl.BlockSpec(memory_space=pl.ANY)
VECTOR = pl.BlockSpec(memory_space=pltpu.VMEM)


def call(kernel, name, shapes, in_specs, out_specs, scratch, products, limit):
    cost = pl.CostEstimate(
        flops=2 * products * 256**3, bytes_accessed=4 * 2**20, transcendentals=0
    )
    return pl.pallas_call(
        kernel,
        out_shape=shapes,
        in_specs=in_specs,
        out_specs=out_specs,
        scratch_shapes=scratch,
        compiler_params=pltpu.CompilerParams(vmem_limit_bytes=limit * 2**20),
        cost_estimate=cost,
        name=name,
    )


def pack(density):
    block = density.shape[2]
    sizes = (PART, MIDDLE, OUTER, WHOLE)
    shapes = [jax.ShapeDtypeStruct((1, size, block, block), density.dtype) for size in sizes]
    return call(pack_kernel, "pack", shapes, [VECTOR], [VECTOR] * len(sizes), [], 1, 8)(density)


def first(own, beside):
    block = own.shape[2]
    shape = jax.ShapeDtypeStruct((BAND, block, block), jnp.float32)
    return call(first_kernel, "first", shape, [VECTOR] * 2, VECTOR, [], 46, 16)(own, beside)


def second(own, far, before):
    block = own.shape[2]
    shapes = [
        jax.ShapeDtypeStruct((BAND, block, block), jnp.float32),
        jax.ShapeDtypeStruct((4 * (MIDDLE + OUTER), block, block), own.dtype),
    ]
    return call(
        second_kernel,
        "second",
        shapes,
        [VECTOR] + [ANYWHERE] * 8 + [VECTOR],
        [VECTOR] * 2,
        [pltpu.SemaphoreType.DMA((8,))],
        30,
        24,
    )(own, *far, before)


def last(keep, own, beside, far, following, before):
    block = own.shape[2]
    shape = jax.ShapeDtypeStruct((1, BAND, block, LANES), jnp.float32)
    return call(
        last_kernel,
        "last",
        shape,
        [SCALARS] + [VECTOR] * 3 + [ANYWHERE] * 6 + [VECTOR],
        ANYWHERE,
        [
            pltpu.VMEM((4 * WHOLE, block, block), own.dtype),
            pltpu.VMEM((BAND, block, block), own.dtype),
            pltpu.VMEM((BAND, block, LANES), jnp.float32),
            pltpu.VMEM((BAND, block, LANES), jnp.float32),
            pltpu.SemaphoreType.DMA((6,)),
            pltpu.SemaphoreType.DMA((BAND,)),
        ],
        120,
        32,
    )(keep, own, beside, far, *following, before)


def after(*arrays):
    return lax.optimization_barrier(arrays)


def body(density, pattern):
    axes = ("row", "col", "layer")
    rows = lax.axis_size(("row", "col"))
    layers = lax.axis_size("layer")
    width = density.shape[2] // layers

    def fetch(array, step):
        pairs = []
        for source in range(rows):
            for plane in range(layers):
                shift = 2 * step * (1 - 2 * (source % 2)) * (1 - 2 * (plane % 2))
                pairs.append((source * layers + plane, (source - shift) % rows * layers + plane))
        return lax.ppermute(array, axes, pairs)

    def fetch_diag(array):
        pairs = []
        for source in range(rows):
            shift = 2 if source // 2 % 2 else -2
            pairs.append((source, (source + shift) % rows))
        return lax.ppermute(array, ("row", "col"), pairs)

    def swap(array, axis, distance):
        peers = lax.axis_size(axis)
        return lax.ppermute(array, axis, [(peer, peer ^ distance) for peer in range(peers)])

    swap_cores = lambda array: swap(array, "col", 1)
    swap_layers = lambda array: swap(array, "layer", 1)

    beside = swap_cores(density)
    diag, middle, outer, pure = pack(density)
    diag = fetch_diag(diag)
    middle = fetch(middle, 2)
    outer = fetch(outer, 3)
    pure = swap(pure, "col", 2)
    sums = first(density, beside)
    sums, middle = after(sums, middle)
    far_middle = swap_layers(middle)
    other_middle = swap_cores(middle)
    middle, outer = after(middle, outer)
    far_outer = swap_layers(outer)
    other_outer = swap_cores(outer)
    outer, diag = after(outer, diag)
    far_diag = swap_layers(diag)
    other_diag = swap_cores(diag)
    diag, far_middle, far_outer, pure = after(diag, far_middle, far_outer, pure)
    other_far_middle = swap_cores(far_middle)
    other_far_outer = swap_cores(far_outer)
    other_pure = swap_cores(pure)
    far = [middle, far_middle, outer, far_outer]
    far = far + [other_middle, other_far_middle, other_outer, other_far_outer]
    sums, far = second(density, far, sums)
    other_far_diag = swap_cores(far_diag)
    following = [pure, diag, far_diag, other_pure, other_diag, other_far_diag]
    out = last(pattern, density, beside, far, following, sums)
    if width < LANES:
        layer = lax.axis_index("layer")
        out = lax.dynamic_slice_in_dim(out, layer * width % LANES, width, 3)
    return out


def solution(mesh):
    return jax.shard_map(
        body,
        mesh=mesh,
        in_specs=(P(("row", "col"), None, None, None), P(("row", "col"), None)),
        out_specs=P(("row", "col"), None, None, "layer"),
        check_vma=False,
    )
```

```python
import jax
import jax.numpy as jnp
from jax import lax
from jax.experimental import pallas as pl
from jax.experimental.pallas import tpu as pltpu
from jax.sharding import PartitionSpec as P

HALF = 6
BAND = 2 * HALF + 1
FORWARD = ((0, 1, 2, 3, 4, 5, -3, -5), (0, 1, 2, 3), (0, 1))
BACKWARD = ((0, 1, 2, 3, 4, -4, -5, -6), (0, 1, 2, -6), (0, 0))
SIZES = tuple(len(part) for part in FORWARD)
WHOLE, MIDDLE, OUTER = SIZES
PART = WHOLE // 2
STARTS = (0, WHOLE, WHOLE + MIDDLE)
FETCHED = sum(SIZES)
LANES = 128
FRAME = range(-HALF, HALF + 1)


def places():
    held = {}
    for offset in FRAME:
        held[0, offset] = offset + HALF
    for offset in FRAME:
        held.setdefault((1, 1 + offset), BAND + offset + HALF)
    slot = 2 * BAND
    for other in (False, True):
        for parts, way in ((FORWARD, 1), (BACKWARD, -1)):
            for step, part in enumerate(parts):
                for offset in part:
                    row = way * 2 * (step + 1)
                    column = row + way * offset
                    if other:
                        row, column = 1 - row, 1 - column
                    if (row, column) not in held and (column, row) not in held:
                        held[row, column] = slot
                    slot += 1
    return held


HELD = places()
def stage(slot):
    if slot < 2 * BAND:
        return 0
    return 1 if WHOLE <= (slot - 2 * BAND) % FETCHED < WHOLE + MIDDLE else 2


def terms(column, stages=(0, 1, 2)):
    plain = {}
    turned = {}
    for row in FRAME:
        if abs(row - column) <= HALF:
            if (row, column) in HELD:
                slot, group = HELD[row, column], plain
            else:
                slot, group = HELD[column, row], turned
            if stage(slot) in stages:
                group[row] = slot
    return plain, turned


def pairs():
    def shared(one, two):
        return sum(len(first.keys() & other.keys()) for first, other in zip(terms(one), terms(two)))

    def best(left):
        if len(left) < 2:
            return 0, [left] if left else []
        choices = []
        for place in range(1, len(left)):
            count, rest = best(left[1:place] + left[place + 1 :])
            choices.append((count + shared(left[0], left[place]), [(left[0], left[place])] + rest))
        if len(left) % 2:
            count, rest = best(left[1:])
            choices.append((count, [(left[0],)] + rest))
        return max(choices, key=lambda choice: choice[0])

    return best(tuple(FRAME))[1]


PAIRS = pairs()


def product(lefts, blocks, turned):
    return lax.dot_general(
        jnp.concatenate(lefts, axis=1),
        jnp.concatenate(blocks, axis=1 if turned else 0),
        (((1,), (1 if turned else 0,)), ((), ())),
        preferred_element_type=jnp.float32,
    )


def column_product(left, block, column, stages):
    total = None
    for turned, group in enumerate(terms(column, stages)):
        if group:
            part = product(
                [left(row) for row in group], [block(slot) for slot in group.values()], turned
            )
            total = part if total is None else total + part
    return total


def part_products(left, part, columns):
    totals = [None] * len(columns)

    def add(place, value):
        totals[place] = value if totals[place] is None else totals[place] + value

    for turned in (0, 1):
        groups = [terms(column)[turned] for column in columns]
        both = [row for row in groups[0] if all(row in group for group in groups)]
        if len(columns) > 1 and both:
            blocks = [
                jnp.concatenate([part(group[row], turned) for group in groups], axis=0 if turned else 1)
                for row in both
            ]
            value = product([left(row) for row in both], blocks, turned)
            for place in range(len(columns)):
                add(place, value[:, place * LANES : (place + 1) * LANES])
        for place, group in enumerate(groups):
            alone = [row for row in group if len(columns) == 1 or row not in both]
            if alone:
                blocks = [part(group[row], turned) for row in alone]
                add(place, product([left(row) for row in alone], blocks, turned))
    return totals


def position():
    row = lax.axis_index(("row", "col"))
    return 1 - 2 * (row % 2), lax.axis_index("layer") % 2, (row + row // 2) % 2


def pack_kernel(density, diag, middle, outer, pure):
    way, layer_kind, row_kind = position()

    def bring(out, item, forward, backward, backwards):
        index = HALF + way * jnp.where(backwards == 0, forward, -backward)
        out[0, item] = density[0, index]

    for item in range(PART):
        forward = jnp.where(layer_kind == 0, FORWARD[0][item], FORWARD[0][PART + item])
        backward = jnp.where(layer_kind == 0, BACKWARD[0][item], BACKWARD[0][PART + item])
        bring(diag, item, forward, backward, row_kind)
    for out, step in ((middle, 1), (outer, 2)):
        for item in range(SIZES[step]):
            bring(out, item, FORWARD[step][item], BACKWARD[step][item], layer_kind)
    for item in range(WHOLE):
        bring(pure, item, FORWARD[0][item], BACKWARD[0][item], 1 - row_kind)


def frame_row(way, array):
    return lambda offset: array[0, HALF + way * offset]


def first_kernel(own, beside, sums):
    way, layer_kind, row_kind = position()
    left = frame_row(way, own)
    right = frame_row(way, beside)
    for column in FRAME:
        block = lambda slot: left(slot - HALF) if slot < BAND else right(slot - BAND - HALF)
        sums[column + HALF] = column_product(left, block, column, (0,))


def middle_place(slot):
    group, item = divmod(slot - 2 * BAND, FETCHED)
    return group * MIDDLE + item - WHOLE


def bundle_kernel(*refs):
    arrays, out = refs[:-1], refs[-1]
    place = 0
    for array in arrays:
        for item in range(array.shape[1]):
            out[0, place] = array[0, item]
            place += 1


def second_kernel(own, near, far, other_near, other_far, before, sums, held, sems):
    way, layer_kind, row_kind = position()
    copies = []
    for other, sources in enumerate(((near, far), (other_near, other_far))):
        for source, kind in zip(sources, (layer_kind, 1 - layer_kind)):
            copies.append(
                pltpu.make_async_copy(
                    source.at[0, pl.ds(0, MIDDLE)],
                    held.at[pl.ds((other * 2 + kind) * MIDDLE, MIDDLE)],
                    sems.at[len(copies)],
                )
            )
    for copy in copies:
        copy.start()
    for copy in copies:
        copy.wait()
    left = frame_row(way, own)
    for column in FRAME:
        block = lambda slot: held[middle_place(slot)]
        total = column_product(left, block, column, (1,))
        sums[column + HALF] = before[column + HALF] + (0.0 if total is None else total)


def last_kernel(keep, own, beside, middle, *refs):
    sources, refs = refs[:6], refs[6:]
    before, out, following, rounded, square, result, sems, out_sems = refs
    way, layer_kind, row_kind = position()
    part = lax.axis_index("layer") * (own.shape[2] // lax.axis_size("layer")) // LANES
    copies = []

    def bring(source, first, size, target):
        copies.append(
            pltpu.make_async_copy(
                source.at[0, pl.ds(first, size)],
                following.at[pl.ds(target, size)],
                sems.at[len(copies)],
            )
        )
        copies[-1].start()

    for other in range(2):
        pure, near, far = sources[other * 3 : other * 3 + 3]
        kind = row_kind if other == 0 else 1 - row_kind
        bring(pure, 0, WHOLE, (other * 2 + kind) * WHOLE)
        base = (other * 2 + 1 - kind) * WHOLE
        bring(near, MIDDLE, PART, base + layer_kind * PART)
        bring(far, 0, PART, base + (1 - layer_kind) * PART)
        base = 4 * WHOLE + other * 2 * OUTER
        bring(near, MIDDLE + PART, OUTER, base + layer_kind * OUTER)
        bring(far, PART, OUTER, base + (1 - layer_kind) * OUTER)
    for copy in copies:
        copy.wait()

    left = frame_row(way, own)

    def next_place(slot):
        group, item = divmod(slot - 2 * BAND, FETCHED)
        if item < WHOLE:
            return group * WHOLE + item
        return 4 * WHOLE + group * OUTER + item - WHOLE - MIDDLE

    for column in FRAME:
        total = column_product(left, lambda slot: following[next_place(slot)], column, (2,))
        total = before[column + HALF] + (0.0 if total is None else total)
        total = total * keep[0, HALF + way * column].astype(jnp.float32)
        rounded[column + HALF] = total.astype(jnp.bfloat16)
        mine = total[:, :LANES]
        for piece in range(1, total.shape[1] // LANES):
            mine = jnp.where(part == piece, total[:, piece * LANES : (piece + 1) * LANES], mine)
        square[column + HALF] = mine

    lanes = pl.ds(pl.multiple_of(part * LANES, LANES), LANES)

    def piece(slot, turned):
        if slot < BAND:
            array, index = own, (0, HALF + way * (slot - HALF))
        elif slot < 2 * BAND:
            array, index = beside, (0, HALF + way * (slot - BAND - HALF))
        elif stage(slot) == 1:
            array, index = middle, (middle_place(slot),)
        else:
            array, index = following, (next_place(slot),)
        return array[(*index, lanes, slice(None)) if turned else (*index, slice(None), lanes)]

    written = []
    for columns in PAIRS:
        totals = part_products(lambda row: rounded[row + HALF], piece, columns)
        for column, total in zip(columns, totals):
            total = total * keep[0, HALF + way * column].astype(jnp.float32)
            result[column + HALF] = 3.0 * square[column + HALF] - 2.0 * total
            copy = pltpu.make_async_copy(
                result.at[column + HALF], out.at[0, HALF + way * column], out_sems.at[column + HALF]
            )
            copy.start()
            written.append(copy)
    for copy in written:
        copy.wait()


SCALARS = pl.BlockSpec(memory_space=pltpu.SMEM)
ANYWHERE = pl.BlockSpec(memory_space=pl.ANY)
VECTOR = pl.BlockSpec(memory_space=pltpu.VMEM)


def call(kernel, name, shapes, in_specs, out_specs, scratch, products, limit):
    cost = pl.CostEstimate(
        flops=2 * products * 256**3, bytes_accessed=4 * 2**20, transcendentals=0
    )
    return pl.pallas_call(
        kernel,
        out_shape=shapes,
        in_specs=in_specs,
        out_specs=out_specs,
        scratch_shapes=scratch,
        compiler_params=pltpu.CompilerParams(vmem_limit_bytes=limit * 2**20),
        cost_estimate=cost,
        name=name,
    )


def pack(density):
    block = density.shape[2]
    sizes = (PART, MIDDLE, OUTER, WHOLE)
    shapes = [jax.ShapeDtypeStruct((1, size, block, block), density.dtype) for size in sizes]
    return call(pack_kernel, "pack", shapes, [VECTOR], [VECTOR] * len(sizes), [], 1, 8)(density)


def first(own, beside):
    block = own.shape[2]
    shape = jax.ShapeDtypeStruct((BAND, block, block), jnp.float32)
    return call(first_kernel, "first", shape, [VECTOR] * 2, VECTOR, [], 46, 16)(own, beside)


def bundle(*arrays):
    shape = list(arrays[0].shape)
    shape[1] = sum(array.shape[1] for array in arrays)
    shape = jax.ShapeDtypeStruct(tuple(shape), arrays[0].dtype)
    return call(bundle_kernel, "bundle", shape, [VECTOR] * len(arrays), VECTOR, [], 1, 4)(*arrays)


def second(own, sources, before):
    block = own.shape[2]
    shapes = [before, jax.ShapeDtypeStruct((4 * MIDDLE, block, block), own.dtype)]
    return call(
        second_kernel,
        "second",
        shapes,
        [VECTOR] + [ANYWHERE] * 4 + [VECTOR],
        [VECTOR] * 2,
        [pltpu.SemaphoreType.DMA((4,))],
        30,
        8,
    )(own, *sources, before)


def last(keep, own, beside, middle, sources, before):
    block = own.shape[2]
    shape = jax.ShapeDtypeStruct((1, BAND, block, LANES), jnp.float32)
    return call(
        last_kernel,
        "last",
        shape,
        [SCALARS] + [VECTOR] * 3 + [ANYWHERE] * 6 + [VECTOR],
        ANYWHERE,
        [
            pltpu.VMEM((4 * (WHOLE + OUTER), block, block), own.dtype),
            pltpu.VMEM((BAND, block, block), own.dtype),
            pltpu.VMEM((BAND, block, LANES), jnp.float32),
            pltpu.VMEM((BAND, block, LANES), jnp.float32),
            pltpu.SemaphoreType.DMA((10,)),
            pltpu.SemaphoreType.DMA((BAND,)),
        ],
        120,
        24,
    )(keep, own, beside, middle, *sources, before)


def after(*arrays):
    return lax.optimization_barrier(arrays)


def body(density, pattern):
    axes = ("row", "col", "layer")
    rows = lax.axis_size(("row", "col"))
    layers = lax.axis_size("layer")
    width = density.shape[2] // layers

    def fetch(array, step):
        pairs = []
        for source in range(rows):
            for plane in range(layers):
                shift = 2 * step * (1 - 2 * (source % 2)) * (1 - 2 * (plane % 2))
                pairs.append((source * layers + plane, (source - shift) % rows * layers + plane))
        return lax.ppermute(array, axes, pairs)

    def fetch_diag(array):
        pairs = []
        for source in range(rows):
            shift = 2 if source // 2 % 2 else -2
            pairs.append((source, (source + shift) % rows))
        return lax.ppermute(array, ("row", "col"), pairs)

    def swap(array, axis, distance):
        peers = lax.axis_size(axis)
        return lax.ppermute(array, axis, [(peer, peer ^ distance) for peer in range(peers)])

    swap_cores = lambda array: swap(array, "col", 1)

    def swap_layers(array):
        peers = lax.axis_size("col")
        pairs = []
        for peer in range(peers):
            for plane in range(layers):
                pairs.append((peer * layers + plane, (peer ^ 1) * layers + (plane ^ 1)))
        return lax.ppermute(array, ("col", "layer"), pairs)

    beside = swap_cores(density)
    diag, middle, outer, pure = pack(density)
    diag = fetch_diag(diag)
    middle = fetch(middle, 2)
    outer = fetch(outer, 3)
    pure = swap(pure, "col", 2)
    sums = first(density, beside)
    sums, middle = after(sums, middle)
    far_middle = swap_layers(middle)
    far_diag = swap_layers(diag)
    far_middle, outer = after(far_middle, outer)
    far_outer = swap_layers(outer)
    near = bundle(middle, diag, outer)
    other_near = swap_cores(near)
    far_diag, pure = after(far_diag, pure)
    own_far_middle = swap_cores(far_middle)
    sums, middle = second(density, [near, own_far_middle, other_near, far_middle], sums)
    other_pure = swap_cores(pure)
    far = bundle(far_diag, far_outer)
    own_far = swap_cores(far)
    sources = [pure, near, own_far, other_pure, other_near, far]
    out = last(pattern, density, beside, middle, sources, sums)
    if width < LANES:
        layer = lax.axis_index("layer")
        out = lax.dynamic_slice_in_dim(out, layer * width % LANES, width, 3)
    return out


def solution(mesh):
    return jax.shard_map(
        body,
        mesh=mesh,
        in_specs=(P(("row", "col"), None, None, None), P(("row", "col"), None)),
        out_specs=P(("row", "col"), None, None, "layer"),
        check_vma=False,
    )
```

```python
import jax
import jax.numpy as jnp
from jax import lax
from jax.experimental import pallas as pl
from jax.experimental.pallas import tpu as pltpu
from jax.sharding import PartitionSpec as P

HALF = 6
BAND = 2 * HALF + 1
FORWARD = ((0, 1, 2, 3, 4, 5, -3, -5), (0, 1, 2, 3), (0, 1))
BACKWARD = ((0, 1, 2, 3, 4, -4, -5, -6), (0, 1, 2, -6), (0, 0))
SIZES = tuple(len(part) for part in FORWARD)
WHOLE, MIDDLE, OUTER = SIZES
PART = WHOLE // 2
STARTS = (0, WHOLE, WHOLE + MIDDLE)
FETCHED = sum(SIZES)
LANES = 128
FRAME = range(-HALF, HALF + 1)


def places():
    held = {}
    for offset in FRAME:
        held[0, offset] = offset + HALF
    for offset in FRAME:
        held.setdefault((1, 1 + offset), BAND + offset + HALF)
    slot = 2 * BAND
    for other in (False, True):
        for parts, way in ((FORWARD, 1), (BACKWARD, -1)):
            for step, part in enumerate(parts):
                for offset in part:
                    row = way * 2 * (step + 1)
                    column = row + way * offset
                    if other:
                        row, column = 1 - row, 1 - column
                    if (row, column) not in held and (column, row) not in held:
                        held[row, column] = slot
                    slot += 1
    return held


HELD = places()
def stage(slot):
    if slot < 2 * BAND:
        return 0
    group, item = divmod(slot - 2 * BAND, FETCHED)
    if item < WHOLE:
        return 2 if group in (0, 3) else 3
    return 1 if item < WHOLE + MIDDLE else 4


def terms(column, stages=(0, 1, 2, 3, 4)):
    plain = {}
    turned = {}
    for row in FRAME:
        if abs(row - column) <= HALF:
            if (row, column) in HELD:
                slot, group = HELD[row, column], plain
            else:
                slot, group = HELD[column, row], turned
            if stage(slot) in stages:
                group[row] = slot
    return plain, turned


def pairs():
    def shared(one, two):
        return sum(len(first.keys() & other.keys()) for first, other in zip(terms(one), terms(two)))

    def best(left):
        if len(left) < 2:
            return 0, [left] if left else []
        choices = []
        for place in range(1, len(left)):
            count, rest = best(left[1:place] + left[place + 1 :])
            choices.append((count + shared(left[0], left[place]), [(left[0], left[place])] + rest))
        if len(left) % 2:
            count, rest = best(left[1:])
            choices.append((count, [(left[0],)] + rest))
        return max(choices, key=lambda choice: choice[0])

    return best(tuple(FRAME))[1]


PAIRS = pairs()


def product(lefts, blocks, turned):
    return lax.dot_general(
        jnp.concatenate(lefts, axis=1),
        jnp.concatenate(blocks, axis=1 if turned else 0),
        (((1,), (1 if turned else 0,)), ((), ())),
        preferred_element_type=jnp.float32,
    )


def column_product(left, block, column, stages):
    total = None
    for turned, group in enumerate(terms(column, stages)):
        if group:
            part = product(
                [left(row) for row in group], [block(slot) for slot in group.values()], turned
            )
            total = part if total is None else total + part
    return total


def part_products(left, part, columns):
    totals = [None] * len(columns)

    def add(place, value):
        totals[place] = value if totals[place] is None else totals[place] + value

    for turned in (0, 1):
        groups = [terms(column)[turned] for column in columns]
        both = [row for row in groups[0] if all(row in group for group in groups)]
        if len(columns) > 1 and both:
            blocks = [
                jnp.concatenate([part(group[row], turned) for group in groups], axis=0 if turned else 1)
                for row in both
            ]
            value = product([left(row) for row in both], blocks, turned)
            for place in range(len(columns)):
                add(place, value[:, place * LANES : (place + 1) * LANES])
        for place, group in enumerate(groups):
            alone = [row for row in group if len(columns) == 1 or row not in both]
            if alone:
                blocks = [part(group[row], turned) for row in alone]
                add(place, product([left(row) for row in alone], blocks, turned))
    return totals


def position():
    row = lax.axis_index(("row", "col"))
    return 1 - 2 * (row % 2), lax.axis_index("layer") % 2, (row + row // 2) % 2


def pack_kernel(density, diag, middle, outer, pure):
    way, layer_kind, row_kind = position()

    def bring(out, item, forward, backward, backwards):
        index = HALF + way * jnp.where(backwards == 0, forward, -backward)
        out[0, item] = density[0, index]

    for item in range(PART):
        forward = jnp.where(layer_kind == 0, FORWARD[0][item], FORWARD[0][PART + item])
        backward = jnp.where(layer_kind == 0, BACKWARD[0][item], BACKWARD[0][PART + item])
        bring(diag, item, forward, backward, row_kind)
    for out, step in ((middle, 1), (outer, 2)):
        for item in range(SIZES[step]):
            bring(out, item, FORWARD[step][item], BACKWARD[step][item], layer_kind)
    for item in range(WHOLE):
        bring(pure, item, FORWARD[0][item], BACKWARD[0][item], 1 - row_kind)


def frame_row(way, array):
    return lambda offset: array[0, HALF + way * offset]


def first_kernel(own, beside, sums):
    way, layer_kind, row_kind = position()
    left = frame_row(way, own)
    right = frame_row(way, beside)
    for column in FRAME:
        block = lambda slot: left(slot - HALF) if slot < BAND else right(slot - BAND - HALF)
        sums[column + HALF] = column_product(left, block, column, (0,))


def middle_place(slot):
    group, item = divmod(slot - 2 * BAND, FETCHED)
    return group * MIDDLE + item - WHOLE


def bundle_kernel(*refs):
    arrays, out = refs[:-1], refs[-1]
    place = 0
    for array in arrays:
        for item in range(array.shape[1]):
            out[0, place] = array[0, item]
            place += 1


def second_kernel(own, near, far, other_near, other_far, before, sums, held, sems):
    way, layer_kind, row_kind = position()
    copies = []
    for other, sources in enumerate(((near, far), (other_near, other_far))):
        for source, kind in zip(sources, (layer_kind, 1 - layer_kind)):
            copies.append(
                pltpu.make_async_copy(
                    source.at[0, pl.ds(0, MIDDLE)],
                    held.at[pl.ds((other * 2 + kind) * MIDDLE, MIDDLE)],
                    sems.at[len(copies)],
                )
            )
    for copy in copies:
        copy.start()
    for copy in copies:
        copy.wait()
    left = frame_row(way, own)
    for column in FRAME:
        block = lambda slot: held[middle_place(slot)]
        total = column_product(left, block, column, (1,))
        sums[column + HALF] = before[column + HALF] + (0.0 if total is None else total)


def third_kernel(own, pure, other_pure, before, sums):
    way, layer_kind, row_kind = position()
    left = frame_row(way, own)
    for kind in (0, 1):

        def block(slot):
            place, item = divmod(slot - 2 * BAND, FETCHED)
            return other_pure[0, item] if place >= 2 else pure[0, item]

        @pl.when(row_kind == kind)
        def _():
            for column in FRAME:
                total = column_product(left, block, column, (2 + kind,))
                sums[column + HALF] = before[column + HALF] + (0.0 if total is None else total)


def last_kernel(keep, own, beside, middle, *refs):
    sources, refs = refs[:6], refs[6:]
    before, out, following, sums, rounded, square, result, sems, out_sems = refs
    way, layer_kind, row_kind = position()
    part = lax.axis_index("layer") * (own.shape[2] // lax.axis_size("layer")) // LANES
    copies = []

    def bring(source, first, size, target):
        copies.append(
            pltpu.make_async_copy(
                source.at[0, pl.ds(first, size)],
                following.at[pl.ds(target, size)],
                sems.at[len(copies)],
            )
        )
        copies[-1].start()

    for other in range(2):
        pure, near, far = sources[other * 3 : other * 3 + 3]
        kind = row_kind if other == 0 else 1 - row_kind
        bring(pure, 0, WHOLE, (other * 2 + kind) * WHOLE)
        base = (other * 2 + 1 - kind) * WHOLE
        bring(near, MIDDLE, PART, base + layer_kind * PART)
        bring(far, 0, PART, base + (1 - layer_kind) * PART)
        base = 4 * WHOLE + other * 2 * OUTER
        bring(near, MIDDLE + PART, OUTER, base + layer_kind * OUTER)
        bring(far, PART, OUTER, base + (1 - layer_kind) * OUTER)
    for copy in copies:
        copy.wait()

    left = frame_row(way, own)

    def next_place(slot):
        group, item = divmod(slot - 2 * BAND, FETCHED)
        if item < WHOLE:
            return group * WHOLE + item
        return 4 * WHOLE + group * OUTER + item - WHOLE - MIDDLE

    for kind in (0, 1):

        @pl.when(row_kind == kind)
        def _():
            block = lambda slot: following[next_place(slot)]
            for column in FRAME:
                total = column_product(left, block, column, (3 - kind, 4))
                sums[column + HALF] = before[column + HALF] + (0.0 if total is None else total)

    for column in FRAME:
        total = sums[column + HALF]
        total = total * keep[0, HALF + way * column].astype(jnp.float32)
        rounded[column + HALF] = total.astype(jnp.bfloat16)
        mine = total[:, :LANES]
        for piece in range(1, total.shape[1] // LANES):
            mine = jnp.where(part == piece, total[:, piece * LANES : (piece + 1) * LANES], mine)
        square[column + HALF] = mine

    lanes = pl.ds(pl.multiple_of(part * LANES, LANES), LANES)

    def piece(slot, turned):
        if slot < BAND:
            array, index = own, (0, HALF + way * (slot - HALF))
        elif slot < 2 * BAND:
            array, index = beside, (0, HALF + way * (slot - BAND - HALF))
        elif stage(slot) == 1:
            array, index = middle, (middle_place(slot),)
        else:
            array, index = following, (next_place(slot),)
        return array[(*index, lanes, slice(None)) if turned else (*index, slice(None), lanes)]

    written = []
    for columns in PAIRS:
        totals = part_products(lambda row: rounded[row + HALF], piece, columns)
        for column, total in zip(columns, totals):
            total = total * keep[0, HALF + way * column].astype(jnp.float32)
            result[column + HALF] = 3.0 * square[column + HALF] - 2.0 * total
            copy = pltpu.make_async_copy(
                result.at[column + HALF], out.at[0, HALF + way * column], out_sems.at[column + HALF]
            )
            copy.start()
            written.append(copy)
    for copy in written:
        copy.wait()


SCALARS = pl.BlockSpec(memory_space=pltpu.SMEM)
ANYWHERE = pl.BlockSpec(memory_space=pl.ANY)
VECTOR = pl.BlockSpec(memory_space=pltpu.VMEM)


def call(kernel, name, shapes, in_specs, out_specs, scratch, products, limit):
    cost = pl.CostEstimate(
        flops=2 * products * 256**3, bytes_accessed=4 * 2**20, transcendentals=0
    )
    return pl.pallas_call(
        kernel,
        out_shape=shapes,
        in_specs=in_specs,
        out_specs=out_specs,
        scratch_shapes=scratch,
        compiler_params=pltpu.CompilerParams(vmem_limit_bytes=limit * 2**20),
        cost_estimate=cost,
        name=name,
    )


def pack(density):
    block = density.shape[2]
    sizes = (PART, MIDDLE, OUTER, WHOLE)
    shapes = [jax.ShapeDtypeStruct((1, size, block, block), density.dtype) for size in sizes]
    return call(pack_kernel, "pack", shapes, [VECTOR], [VECTOR] * len(sizes), [], 1, 8)(density)


def first(own, beside):
    block = own.shape[2]
    shape = jax.ShapeDtypeStruct((BAND, block, block), jnp.float32)
    return call(first_kernel, "first", shape, [VECTOR] * 2, VECTOR, [], 46, 16)(own, beside)


def bundle(*arrays):
    shape = list(arrays[0].shape)
    shape[1] = sum(array.shape[1] for array in arrays)
    shape = jax.ShapeDtypeStruct(tuple(shape), arrays[0].dtype)
    return call(bundle_kernel, "bundle", shape, [VECTOR] * len(arrays), VECTOR, [], 1, 4)(*arrays)


def second(own, sources, before):
    block = own.shape[2]
    shapes = [before, jax.ShapeDtypeStruct((4 * MIDDLE, block, block), own.dtype)]
    return call(
        second_kernel,
        "second",
        shapes,
        [VECTOR] + [ANYWHERE] * 4 + [VECTOR],
        [VECTOR] * 2,
        [pltpu.SemaphoreType.DMA((4,))],
        30,
        8,
    )(own, *sources, before)


def third(own, pure, other_pure, before):
    return call(third_kernel, "third", before, [VECTOR] * 4, VECTOR, [], 30, 8)(
        own, pure, other_pure, before
    )


def last(keep, own, beside, middle, sources, before):
    block = own.shape[2]
    shape = jax.ShapeDtypeStruct((1, BAND, block, LANES), jnp.float32)
    return call(
        last_kernel,
        "last",
        shape,
        [SCALARS] + [VECTOR] * 3 + [ANYWHERE] * 6 + [VECTOR],
        ANYWHERE,
        [
            pltpu.VMEM((4 * (WHOLE + OUTER), block, block), own.dtype),
            pltpu.VMEM((BAND, block, block), jnp.float32),
            pltpu.VMEM((BAND, block, block), own.dtype),
            pltpu.VMEM((BAND, block, LANES), jnp.float32),
            pltpu.VMEM((BAND, block, LANES), jnp.float32),
            pltpu.SemaphoreType.DMA((10,)),
            pltpu.SemaphoreType.DMA((BAND,)),
        ],
        120,
        24,
    )(keep, own, beside, middle, *sources, before)


def after(*arrays):
    return lax.optimization_barrier(arrays)


def body(density, pattern):
    axes = ("row", "col", "layer")
    rows = lax.axis_size(("row", "col"))
    layers = lax.axis_size("layer")
    width = density.shape[2] // layers

    def fetch(array, step):
        pairs = []
        for source in range(rows):
            for plane in range(layers):
                shift = 2 * step * (1 - 2 * (source % 2)) * (1 - 2 * (plane % 2))
                pairs.append((source * layers + plane, (source - shift) % rows * layers + plane))
        return lax.ppermute(array, axes, pairs)

    def fetch_diag(array):
        pairs = []
        for source in range(rows):
            shift = 2 if source // 2 % 2 else -2
            pairs.append((source, (source + shift) % rows))
        return lax.ppermute(array, ("row", "col"), pairs)

    def swap(array, axis, distance):
        peers = lax.axis_size(axis)
        return lax.ppermute(array, axis, [(peer, peer ^ distance) for peer in range(peers)])

    swap_cores = lambda array: swap(array, "col", 1)

    def swap_layers(array):
        peers = lax.axis_size("col")
        pairs = []
        for peer in range(peers):
            for plane in range(layers):
                pairs.append((peer * layers + plane, (peer ^ 1) * layers + (plane ^ 1)))
        return lax.ppermute(array, ("col", "layer"), pairs)

    beside = swap_cores(density)
    diag, middle, outer, pure = pack(density)
    diag = fetch_diag(diag)
    middle = fetch(middle, 2)
    outer = fetch(outer, 3)
    pure = swap(pure, "col", 2)
    sums = first(density, beside)
    sums, middle = after(sums, middle)
    far_middle = swap_layers(middle)
    far_diag = swap_layers(diag)
    far_middle, outer = after(far_middle, outer)
    far_outer = swap_layers(outer)
    near = bundle(middle, diag, outer)
    other_near = swap_cores(near)
    own_far_middle = swap_cores(bundle(far_middle, far_middle))
    sums, middle = second(density, [near, own_far_middle, other_near, far_middle], sums)
    far_outer, far_diag, pure = after(far_outer, far_diag, pure)
    other_pure = swap_cores(pure)
    sums = third(density, pure, other_pure, sums)
    far = bundle(far_diag, far_outer)
    own_far = swap_cores(far)
    sources = [pure, near, own_far, other_pure, other_near, far]
    out = last(pattern, density, beside, middle, sources, sums)
    if width < LANES:
        layer = lax.axis_index("layer")
        out = lax.dynamic_slice_in_dim(out, layer * width % LANES, width, 3)
    return out


def solution(mesh):
    return jax.shard_map(
        body,
        mesh=mesh,
        in_specs=(P(("row", "col"), None, None, None), P(("row", "col"), None)),
        out_specs=P(("row", "col"), None, None, "layer"),
        check_vma=False,
    )
```

```python
import jax
import jax.numpy as jnp
from jax import lax
from jax.experimental import pallas as pl
from jax.experimental.pallas import tpu as pltpu
from jax.sharding import PartitionSpec as P

HALF = 6
BAND = 2 * HALF + 1
FORWARD = ((0, 1, 2, 3, 4, 5, -3, -5), (0, 1, 2, 3), (0, 1))
BACKWARD = ((0, 1, 2, 3, 4, -4, -5, -6), (0, 1, 2, -6), (0, 0))
SIZES = tuple(len(part) for part in FORWARD)
WHOLE, MIDDLE, OUTER = SIZES
LEFT_OUT = 6
PARTS = ((0, 1, 2), (3, 4, 5, 7))
PART = len(PARTS[1])
SENT = len(PARTS[0])
STARTS = (0, WHOLE, WHOLE + MIDDLE)
FETCHED = sum(SIZES)
LANES = 128
FRAME = range(-HALF, HALF + 1)


def places():
    held = {}
    for offset in FRAME:
        held[0, offset] = offset + HALF
    for offset in FRAME:
        held.setdefault((1, 1 + offset), BAND + offset + HALF)
    slot = 2 * BAND
    for other in (False, True):
        for parts, way in ((FORWARD, 1), (BACKWARD, -1)):
            for step, part in enumerate(parts):
                for offset in part:
                    row = way * 2 * (step + 1)
                    column = row + way * offset
                    if other:
                        row, column = 1 - row, 1 - column
                    if (row, column) not in held and (column, row) not in held:
                        held[row, column] = slot
                    slot += 1
    return held


HELD = places()
def stage(slot):
    if slot < 2 * BAND:
        return 0
    group, item = divmod(slot - 2 * BAND, FETCHED)
    if item < WHOLE:
        return 2 if group in (0, 3) else 3
    return 1 if item < WHOLE + MIDDLE else 4


def terms(column, stages=(0, 1, 2, 3, 4)):
    plain = {}
    turned = {}
    for row in FRAME:
        if abs(row - column) <= HALF:
            if (row, column) in HELD:
                slot, group = HELD[row, column], plain
            else:
                slot, group = HELD[column, row], turned
            if stage(slot) in stages:
                group[row] = slot
    return plain, turned


def pairs():
    def shared(one, two):
        return sum(len(first.keys() & other.keys()) for first, other in zip(terms(one), terms(two)))

    def best(left):
        if len(left) < 2:
            return 0, [left] if left else []
        choices = []
        for place in range(1, len(left)):
            count, rest = best(left[1:place] + left[place + 1 :])
            choices.append((count + shared(left[0], left[place]), [(left[0], left[place])] + rest))
        if len(left) % 2:
            count, rest = best(left[1:])
            choices.append((count, [(left[0],)] + rest))
        return max(choices, key=lambda choice: choice[0])

    return best(tuple(FRAME))[1]


PAIRS = pairs()


def product(lefts, blocks, turned):
    return lax.dot_general(
        jnp.concatenate(lefts, axis=1),
        jnp.concatenate(blocks, axis=1 if turned else 0),
        (((1,), (1 if turned else 0,)), ((), ())),
        preferred_element_type=jnp.float32,
    )


def column_product(left, block, column, stages):
    total = None
    for turned, group in enumerate(terms(column, stages)):
        if group:
            part = product(
                [left(row) for row in group], [block(slot) for slot in group.values()], turned
            )
            total = part if total is None else total + part
    return total


def part_products(left, part, columns):
    totals = [None] * len(columns)

    def add(place, value):
        totals[place] = value if totals[place] is None else totals[place] + value

    for turned in (0, 1):
        groups = [terms(column)[turned] for column in columns]
        both = [row for row in groups[0] if all(row in group for group in groups)]
        if len(columns) > 1 and both:
            blocks = [
                jnp.concatenate([part(group[row], turned) for group in groups], axis=0 if turned else 1)
                for row in both
            ]
            value = product([left(row) for row in both], blocks, turned)
            for place in range(len(columns)):
                add(place, value[:, place * LANES : (place + 1) * LANES])
        for place, group in enumerate(groups):
            alone = [row for row in group if len(columns) == 1 or row not in both]
            if alone:
                blocks = [part(group[row], turned) for row in alone]
                add(place, product([left(row) for row in alone], blocks, turned))
    return totals


def position():
    row = lax.axis_index(("row", "col"))
    return 1 - 2 * (row % 2), lax.axis_index("layer") % 2, (row + row // 2) % 2


def pack_kernel(density, diag, middle, outer, pure):
    way, layer_kind, row_kind = position()

    def bring(out, item, forward, backward, backwards):
        index = HALF + way * jnp.where(backwards == 0, forward, -backward)
        out[0, item] = density[0, index]

    for item in range(PART):
        one, other = PARTS[0][min(item, SENT - 1)], PARTS[1][item]
        forward = jnp.where(layer_kind == 0, FORWARD[0][one], FORWARD[0][other])
        backward = jnp.where(layer_kind == 0, BACKWARD[0][one], BACKWARD[0][other])
        bring(diag, item, forward, backward, row_kind)
    for out, step in ((middle, 1), (outer, 2)):
        for item in range(SIZES[step]):
            bring(out, item, FORWARD[step][item], BACKWARD[step][item], layer_kind)
    for item in range(WHOLE):
        bring(pure, item, FORWARD[0][item], BACKWARD[0][item], 1 - row_kind)


def frame_row(way, array):
    return lambda offset: array[0, HALF + way * offset]


def first_kernel(own, beside, sums):
    way, layer_kind, row_kind = position()
    left = frame_row(way, own)
    right = frame_row(way, beside)
    for column in FRAME:
        block = lambda slot: left(slot - HALF) if slot < BAND else right(slot - BAND - HALF)
        sums[column + HALF] = column_product(left, block, column, (0,))


def middle_place(slot):
    group, item = divmod(slot - 2 * BAND, FETCHED)
    return group * MIDDLE + item - WHOLE


def bundle_kernel(*refs):
    arrays, out = refs[:-1], refs[-1]
    place = 0
    for array in arrays:
        for item in range(array.shape[1]):
            out[0, place] = array[0, item]
            place += 1


def swap_kernel(diag, out):
    for item in range(SENT):
        out[0, item] = diag[0, item]


def rest_kernel(diag, outer, out):
    way, layer_kind, row_kind = position()

    @pl.when(layer_kind == 0)
    def _():
        for item in range(OUTER):
            out[0, item] = outer[0, item]

    @pl.when(layer_kind == 1)
    def _():
        out[0, 0] = diag[0, SENT]
        out[0, 1] = outer[0, 0]


def second_kernel(own, near, far, other_near, other_far, before, sums, held, sems):
    way, layer_kind, row_kind = position()
    copies = []
    for other, sources in enumerate(((near, far), (other_near, other_far))):
        for source, kind in zip(sources, (layer_kind, 1 - layer_kind)):
            copies.append(
                pltpu.make_async_copy(
                    source.at[0, pl.ds(0, MIDDLE)],
                    held.at[pl.ds((other * 2 + kind) * MIDDLE, MIDDLE)],
                    sems.at[len(copies)],
                )
            )
    for copy in copies:
        copy.start()
    for copy in copies:
        copy.wait()
    left = frame_row(way, own)
    for column in FRAME:
        block = lambda slot: held[middle_place(slot)]
        total = column_product(left, block, column, (1,))
        sums[column + HALF] = before[column + HALF] + (0.0 if total is None else total)


def third_kernel(own, pure, other_pure, before, sums, turned):
    way, layer_kind, row_kind = position()
    turned[0] = other_pure[0, LEFT_OUT].T
    left = frame_row(way, own)
    for kind in (0, 1):

        def block(slot):
            place, item = divmod(slot - 2 * BAND, FETCHED)
            return other_pure[0, item] if place >= 2 else pure[0, item]

        @pl.when(row_kind == kind)
        def _():
            for column in FRAME:
                total = column_product(left, block, column, (2 + kind,))
                sums[column + HALF] = before[column + HALF] + (0.0 if total is None else total)


def last_kernel(keep, own, beside, middle, *refs):
    sources, refs = refs[:6], refs[6:]
    turned, before, out, following, rounded, square, result, out_sems = refs
    way, layer_kind, row_kind = position()
    part = lax.axis_index("layer") * (own.shape[2] // lax.axis_size("layer")) // LANES

    def bring(source, first, size, target):
        for item in range(size):
            following[target + item] = source[0, first + item]

    for other in range(2):
        pure, near, far = sources[other * 3 : other * 3 + 3]
        kind = row_kind if other == 0 else 1 - row_kind
        bring(pure, 0, WHOLE, (other * 2 + kind) * WHOLE)
        base = (other * 2 + 1 - kind) * WHOLE
        last_item = base + PARTS[1][-1]
        ends = (4 * WHOLE + other * 2 * OUTER, 4 * WHOLE + (other * 2 + 1) * OUTER)
        even = layer_kind == 0
        spare = 4 * (WHOLE + OUTER) + other
        bring(near, MIDDLE, SENT, base + layer_kind * SENT)
        bring(far, 0, SENT, base + (1 - layer_kind) * SENT)
        following[jnp.where(even, spare, last_item)] = near[0, MIDDLE + SENT]
        for item in range(OUTER):
            following[jnp.where(even, *ends) + item] = near[0, MIDDLE + PART + item]
        following[jnp.where(even, last_item, ends[0])] = far[0, SENT]
        following[jnp.where(even, ends[1], ends[0] + 1)] = far[0, SENT + 1]
    following[(1 - row_kind) * WHOLE + LEFT_OUT] = turned[0]

    left = frame_row(way, own)

    def next_place(slot):
        group, item = divmod(slot - 2 * BAND, FETCHED)
        if item < WHOLE:
            return group * WHOLE + item
        return 4 * WHOLE + group * OUTER + item - WHOLE - MIDDLE

    for kind in (0, 1):

        @pl.when(row_kind == kind)
        def _():
            block = lambda slot: following[next_place(slot)]
            for column in FRAME:
                total = column_product(left, block, column, (3 - kind, 4))
                total = before[column + HALF] + (0.0 if total is None else total)
                total = total * keep[0, HALF + way * column].astype(jnp.float32)
                rounded[column + HALF] = total.astype(jnp.bfloat16)
                mine = total[:, :LANES]
                for piece in range(1, total.shape[1] // LANES):
                    lanes = slice(piece * LANES, (piece + 1) * LANES)
                    mine = jnp.where(part == piece, total[:, lanes], mine)
                square[column + HALF] = mine

    lanes = pl.ds(pl.multiple_of(part * LANES, LANES), LANES)

    def piece(slot, turned):
        if slot < BAND:
            array, index = own, (0, HALF + way * (slot - HALF))
        elif slot < 2 * BAND:
            array, index = beside, (0, HALF + way * (slot - BAND - HALF))
        elif stage(slot) == 1:
            array, index = middle, (middle_place(slot),)
        else:
            array, index = following, (next_place(slot),)
        return array[(*index, lanes, slice(None)) if turned else (*index, slice(None), lanes)]

    written = []
    for columns in PAIRS:
        totals = part_products(lambda row: rounded[row + HALF], piece, columns)
        for column, total in zip(columns, totals):
            total = total * keep[0, HALF + way * column].astype(jnp.float32)
            result[column + HALF] = 3.0 * square[column + HALF] - 2.0 * total
            copy = pltpu.make_async_copy(
                result.at[column + HALF], out.at[0, HALF + way * column], out_sems.at[column + HALF]
            )
            copy.start()
            written.append(copy)
    for copy in written:
        copy.wait()


SCALARS = pl.BlockSpec(memory_space=pltpu.SMEM)
ANYWHERE = pl.BlockSpec(memory_space=pl.ANY)
VECTOR = pl.BlockSpec(memory_space=pltpu.VMEM)


def call(kernel, name, shapes, in_specs, out_specs, scratch, products, limit):
    cost = pl.CostEstimate(
        flops=2 * products * 256**3, bytes_accessed=4 * 2**20, transcendentals=0
    )
    return pl.pallas_call(
        kernel,
        out_shape=shapes,
        in_specs=in_specs,
        out_specs=out_specs,
        scratch_shapes=scratch,
        compiler_params=pltpu.CompilerParams(vmem_limit_bytes=limit * 2**20),
        cost_estimate=cost,
        name=name,
    )


def pack(density):
    block = density.shape[2]
    sizes = (PART, MIDDLE, OUTER, WHOLE)
    shapes = [jax.ShapeDtypeStruct((1, size, block, block), density.dtype) for size in sizes]
    return call(pack_kernel, "pack", shapes, [VECTOR], [VECTOR] * len(sizes), [], 1, 8)(density)


def first(own, beside):
    block = own.shape[2]
    shape = jax.ShapeDtypeStruct((BAND, block, block), jnp.float32)
    return call(first_kernel, "first", shape, [VECTOR] * 2, VECTOR, [], 46, 16)(own, beside)


def bundle(*arrays):
    shape = list(arrays[0].shape)
    shape[1] = sum(array.shape[1] for array in arrays)
    shape = jax.ShapeDtypeStruct(tuple(shape), arrays[0].dtype)
    return call(bundle_kernel, "bundle", shape, [VECTOR] * len(arrays), VECTOR, [], 1, 4)(*arrays)


def cut(kernel, size, *arrays):
    shape = list(arrays[0].shape)
    shape[1] = size
    shape = jax.ShapeDtypeStruct(tuple(shape), arrays[0].dtype)
    return call(kernel, "cut", shape, [VECTOR] * len(arrays), VECTOR, [], 1, 4)(*arrays)


def second(own, sources, before):
    block = own.shape[2]
    shapes = [before, jax.ShapeDtypeStruct((4 * MIDDLE, block, block), own.dtype)]
    return call(
        second_kernel,
        "second",
        shapes,
        [VECTOR] + [ANYWHERE] * 4 + [VECTOR],
        [VECTOR] * 2,
        [pltpu.SemaphoreType.DMA((4,))],
        30,
        8,
    )(own, *sources, before)


def third(own, pure, other_pure, before):
    block = own.shape[2]
    shapes = [before, jax.ShapeDtypeStruct((1, block, block), own.dtype)]
    return call(third_kernel, "third", shapes, [VECTOR] * 4, [VECTOR] * 2, [], 30, 8)(
        own, pure, other_pure, before
    )


def last(keep, own, beside, middle, sources, turned, before):
    block = own.shape[2]
    shape = jax.ShapeDtypeStruct((1, BAND, block, LANES), jnp.float32)
    return call(
        last_kernel,
        "last",
        shape,
        [SCALARS] + [VECTOR] * 11,
        ANYWHERE,
        [
            pltpu.VMEM((4 * (WHOLE + OUTER) + 2, block, block), own.dtype),
            pltpu.VMEM((BAND, block, block), own.dtype),
            pltpu.VMEM((BAND, block, LANES), jnp.float32),
            pltpu.VMEM((BAND, block, LANES), jnp.float32),
            pltpu.SemaphoreType.DMA((BAND,)),
        ],
        120,
        24,
    )(keep, own, beside, middle, *sources, turned, before)


def after(*arrays):
    return lax.optimization_barrier(arrays)


def body(density, pattern):
    axes = ("row", "col", "layer")
    rows = lax.axis_size(("row", "col"))
    layers = lax.axis_size("layer")
    width = density.shape[2] // layers

    def fetch(array, step):
        pairs = []
        for source in range(rows):
            for plane in range(layers):
                shift = 2 * step * (1 - 2 * (source % 2)) * (1 - 2 * (plane % 2))
                pairs.append((source * layers + plane, (source - shift) % rows * layers + plane))
        return lax.ppermute(array, axes, pairs)

    def fetch_diag(array):
        pairs = []
        for source in range(rows):
            shift = 2 if source // 2 % 2 else -2
            pairs.append((source, (source + shift) % rows))
        return lax.ppermute(array, ("row", "col"), pairs)

    def swap(array, axis, distance):
        peers = lax.axis_size(axis)
        return lax.ppermute(array, axis, [(peer, peer ^ distance) for peer in range(peers)])

    swap_cores = lambda array: swap(array, "col", 1)

    def swap_layers(array):
        peers = lax.axis_size("col")
        pairs = []
        for peer in range(peers):
            for plane in range(layers):
                pairs.append((peer * layers + plane, (peer ^ 1) * layers + (plane ^ 1)))
        return lax.ppermute(array, ("col", "layer"), pairs)

    beside = swap_cores(density)
    diag, middle, outer, pure = pack(density)
    diag = fetch_diag(diag)
    middle = fetch(middle, 2)
    outer = fetch(outer, 3)
    pure = swap(pure, "col", 2)
    sums = first(density, beside)
    sums, middle = after(sums, middle)
    far_middle = swap_layers(middle)
    far_diag = swap_layers(cut(swap_kernel, SENT, diag))
    far_middle, outer = after(far_middle, outer)
    far_outer = swap_layers(cut(rest_kernel, OUTER, diag, outer))
    near = bundle(middle, diag, outer)
    other_near = swap_cores(near)
    own_far_middle = swap_cores(bundle(far_middle, far_middle))
    sums, middle = second(density, [near, own_far_middle, other_near, far_middle], sums)
    far_outer, far_diag, pure = after(far_outer, far_diag, pure)
    other_pure = swap_cores(pure)
    sums, turned = third(density, pure, other_pure, sums)
    far = bundle(far_diag, far_outer)
    own_far = swap_cores(far)
    sources = [pure, near, own_far, other_pure, other_near, far]
    out = last(pattern, density, beside, middle, sources, turned, sums)
    if width < LANES:
        layer = lax.axis_index("layer")
        out = lax.dynamic_slice_in_dim(out, layer * width % LANES, width, 3)
    return out


def solution(mesh):
    return jax.shard_map(
        body,
        mesh=mesh,
        in_specs=(P(("row", "col"), None, None, None), P(("row", "col"), None)),
        out_specs=P(("row", "col"), None, None, "layer"),
        check_vma=False,
    )
```

```python
import jax
import jax.numpy as jnp
from jax import lax
from jax.experimental import pallas as pl
from jax.experimental.pallas import tpu as pltpu
from jax.sharding import PartitionSpec as P

HALF = 6
BAND = 2 * HALF + 1
FORWARD = ((0, 1, 2, 3, 4, 5, -3, -5), (0, 1, 2, 3), (0, 1))
BACKWARD = ((0, 1, 2, 3, 4, -4, -5, -6), (0, 1, 2, -6), (0, 0))
SIZES = tuple(len(part) for part in FORWARD)
WHOLE, MIDDLE, OUTER = SIZES
LEFT_OUT = 6
PARTS = ((0, 1, 2), (3, 4, 5, 7))
PART = len(PARTS[1])
SENT = len(PARTS[0])
STARTS = (0, WHOLE, WHOLE + MIDDLE)
FETCHED = sum(SIZES)
LANES = 128
FRAME = range(-HALF, HALF + 1)


def places():
    held = {}
    for offset in FRAME:
        held[0, offset] = offset + HALF
    for offset in FRAME:
        held.setdefault((1, 1 + offset), BAND + offset + HALF)
    slot = 2 * BAND
    for other in (False, True):
        for parts, way in ((FORWARD, 1), (BACKWARD, -1)):
            for step, part in enumerate(parts):
                for offset in part:
                    row = way * 2 * (step + 1)
                    column = row + way * offset
                    if other:
                        row, column = 1 - row, 1 - column
                    if (row, column) not in held and (column, row) not in held:
                        held[row, column] = slot
                    slot += 1
    return held


HELD = places()
def stage(slot):
    if slot < 2 * BAND:
        return 0
    group, item = divmod(slot - 2 * BAND, FETCHED)
    if item < WHOLE:
        return 2 if group in (0, 3) else 3
    return 1 if item < WHOLE + MIDDLE else 4


def terms(column, stages=(0, 1, 2, 3, 4)):
    plain = {}
    turned = {}
    for row in FRAME:
        if abs(row - column) <= HALF:
            if (row, column) in HELD:
                slot, group = HELD[row, column], plain
            else:
                slot, group = HELD[column, row], turned
            if stage(slot) in stages:
                group[row] = slot
    return plain, turned


def pairs():
    def shared(one, two):
        return sum(len(first.keys() & other.keys()) for first, other in zip(terms(one), terms(two)))

    def best(left):
        if len(left) < 2:
            return 0, [left] if left else []
        choices = []
        for place in range(1, len(left)):
            count, rest = best(left[1:place] + left[place + 1 :])
            choices.append((count + shared(left[0], left[place]), [(left[0], left[place])] + rest))
        if len(left) % 2:
            count, rest = best(left[1:])
            choices.append((count, [(left[0],)] + rest))
        return max(choices, key=lambda choice: choice[0])

    return best(tuple(FRAME))[1]


PAIRS = pairs()


def product(lefts, blocks, turned):
    return lax.dot_general(
        jnp.concatenate(lefts, axis=1),
        jnp.concatenate(blocks, axis=1 if turned else 0),
        (((1,), (1 if turned else 0,)), ((), ())),
        preferred_element_type=jnp.float32,
    )


def column_product(left, block, column, stages):
    total = None
    for turned, group in enumerate(terms(column, stages)):
        if group:
            part = product(
                [left(row) for row in group], [block(slot) for slot in group.values()], turned
            )
            total = part if total is None else total + part
    return total


def part_products(left, part, columns):
    totals = [None] * len(columns)

    def add(place, value):
        totals[place] = value if totals[place] is None else totals[place] + value

    for turned in (0, 1):
        groups = [terms(column)[turned] for column in columns]
        both = [row for row in groups[0] if all(row in group for group in groups)]
        if len(columns) > 1 and both:
            blocks = [
                jnp.concatenate([part(group[row], turned) for group in groups], axis=0 if turned else 1)
                for row in both
            ]
            value = product([left(row) for row in both], blocks, turned)
            for place in range(len(columns)):
                add(place, value[:, place * LANES : (place + 1) * LANES])
        for place, group in enumerate(groups):
            alone = [row for row in group if len(columns) == 1 or row not in both]
            if alone:
                blocks = [part(group[row], turned) for row in alone]
                add(place, product([left(row) for row in alone], blocks, turned))
    return totals


def position():
    row = lax.axis_index(("row", "col"))
    return 1 - 2 * (row % 2), lax.axis_index("layer") % 2, (row + row // 2) % 2


def pack_kernel(density, diag, middle, outer, pure):
    way, layer_kind, row_kind = position()

    def bring(out, item, forward, backward, backwards):
        index = HALF + way * jnp.where(backwards == 0, forward, -backward)
        out[0, item] = density[0, index]

    for item in range(PART):
        one, other = PARTS[0][min(item, SENT - 1)], PARTS[1][item]
        forward = jnp.where(layer_kind == 0, FORWARD[0][one], FORWARD[0][other])
        backward = jnp.where(layer_kind == 0, BACKWARD[0][one], BACKWARD[0][other])
        bring(diag, item, forward, backward, row_kind)
    for out, step in ((middle, 1), (outer, 2)):
        for item in range(SIZES[step]):
            bring(out, item, FORWARD[step][item], BACKWARD[step][item], layer_kind)
    for item in range(WHOLE):
        bring(pure, item, FORWARD[0][item], BACKWARD[0][item], 1 - row_kind)


def frame_row(way, array):
    return lambda offset: array[0, HALF + way * offset]


def first_kernel(own, beside, sums):
    way, layer_kind, row_kind = position()
    left = frame_row(way, own)
    right = frame_row(way, beside)
    for column in FRAME:
        block = lambda slot: left(slot - HALF) if slot < BAND else right(slot - BAND - HALF)
        sums[column + HALF] = column_product(left, block, column, (0,))


def middle_place(slot):
    group, item = divmod(slot - 2 * BAND, FETCHED)
    return group * MIDDLE + item - WHOLE


def bundle_kernel(*refs):
    arrays, out = refs[:-1], refs[-1]
    place = 0
    for array in arrays:
        for item in range(array.shape[1]):
            out[0, place] = array[0, item]
            place += 1


def swap_kernel(diag, out):
    for item in range(SENT):
        out[0, item] = diag[0, item]


def rest_kernel(diag, outer, out):
    way, layer_kind, row_kind = position()

    @pl.when(layer_kind == 0)
    def _():
        for item in range(OUTER):
            out[0, item] = outer[0, item]

    @pl.when(layer_kind == 1)
    def _():
        out[0, 0] = diag[0, SENT]
        out[0, 1] = outer[0, 0]


def second_kernel(own, near, far, other_near, other_far, before, sums, held, sems):
    way, layer_kind, row_kind = position()
    copies = []
    for other, sources in enumerate(((near, far), (other_near, other_far))):
        for source, kind in zip(sources, (layer_kind, 1 - layer_kind)):
            copies.append(
                pltpu.make_async_copy(
                    source.at[0, pl.ds(0, MIDDLE)],
                    held.at[pl.ds((other * 2 + kind) * MIDDLE, MIDDLE)],
                    sems.at[len(copies)],
                )
            )
    for copy in copies:
        copy.start()
    for copy in copies:
        copy.wait()
    left = frame_row(way, own)
    for column in FRAME:
        block = lambda slot: held[middle_place(slot)]
        total = column_product(left, block, column, (1,))
        sums[column + HALF] = before[column + HALF] + (0.0 if total is None else total)


def third_kernel(own, pure, other_pure, before, sums, turned):
    way, layer_kind, row_kind = position()
    turned[0] = other_pure[0, LEFT_OUT].T
    left = frame_row(way, own)
    for kind in (0, 1):

        def block(slot):
            place, item = divmod(slot - 2 * BAND, FETCHED)
            return other_pure[0, item] if place >= 2 else pure[0, item]

        @pl.when(row_kind == kind)
        def _():
            for column in FRAME:
                total = column_product(left, block, column, (2 + kind,))
                sums[column + HALF] = before[column + HALF] + (0.0 if total is None else total)


def last_kernel(keep, own, beside, middle, *refs):
    sources, outers, refs = refs[:6], refs[6:8], refs[8:]
    turned, before, out, following, rounded, square, result, out_sems = refs
    way, layer_kind, row_kind = position()
    part = lax.axis_index("layer") * (own.shape[2] // lax.axis_size("layer")) // LANES

    def bring(source, first, size, target):
        for item in range(size):
            following[target + item] = source[0, first + item]

    for other in range(2):
        pure, near, far = sources[other * 3 : other * 3 + 3]
        kind = row_kind if other == 0 else 1 - row_kind
        bring(pure, 0, WHOLE, (other * 2 + kind) * WHOLE)
        base = (other * 2 + 1 - kind) * WHOLE
        last_item = base + PARTS[1][-1]
        ends = (4 * WHOLE + other * 2 * OUTER, 4 * WHOLE + (other * 2 + 1) * OUTER)
        even = layer_kind == 0
        spare = 4 * (WHOLE + OUTER) + other
        bring(near, MIDDLE, SENT, base + layer_kind * SENT)
        bring(far, 0, SENT, base + (1 - layer_kind) * SENT)
        following[jnp.where(even, spare, last_item)] = near[0, MIDDLE + SENT]
        for item in range(OUTER):
            following[jnp.where(even, *ends) + item] = outers[other][0, MIDDLE + item]
        following[jnp.where(even, last_item, ends[0])] = far[0, SENT]
        following[jnp.where(even, ends[1], ends[0] + 1)] = far[0, SENT + 1]
    following[(1 - row_kind) * WHOLE + LEFT_OUT] = turned[0]

    left = frame_row(way, own)

    def next_place(slot):
        group, item = divmod(slot - 2 * BAND, FETCHED)
        if item < WHOLE:
            return group * WHOLE + item
        return 4 * WHOLE + group * OUTER + item - WHOLE - MIDDLE

    for kind in (0, 1):

        @pl.when(row_kind == kind)
        def _():
            block = lambda slot: following[next_place(slot)]
            for column in FRAME:
                total = column_product(left, block, column, (3 - kind, 4))
                total = before[column + HALF] + (0.0 if total is None else total)
                total = total * keep[0, HALF + way * column].astype(jnp.float32)
                rounded[column + HALF] = total.astype(jnp.bfloat16)
                mine = total[:, :LANES]
                for piece in range(1, total.shape[1] // LANES):
                    lanes = slice(piece * LANES, (piece + 1) * LANES)
                    mine = jnp.where(part == piece, total[:, lanes], mine)
                square[column + HALF] = mine

    lanes = pl.ds(pl.multiple_of(part * LANES, LANES), LANES)

    def piece(slot, turned):
        if slot < BAND:
            array, index = own, (0, HALF + way * (slot - HALF))
        elif slot < 2 * BAND:
            array, index = beside, (0, HALF + way * (slot - BAND - HALF))
        elif stage(slot) == 1:
            array, index = middle, (middle_place(slot),)
        else:
            array, index = following, (next_place(slot),)
        return array[(*index, lanes, slice(None)) if turned else (*index, slice(None), lanes)]

    written = []
    for columns in PAIRS:
        totals = part_products(lambda row: rounded[row + HALF], piece, columns)
        for column, total in zip(columns, totals):
            total = total * keep[0, HALF + way * column].astype(jnp.float32)
            result[column + HALF] = 3.0 * square[column + HALF] - 2.0 * total
            copy = pltpu.make_async_copy(
                result.at[column + HALF], out.at[0, HALF + way * column], out_sems.at[column + HALF]
            )
            copy.start()
            written.append(copy)
    for copy in written:
        copy.wait()


SCALARS = pl.BlockSpec(memory_space=pltpu.SMEM)
ANYWHERE = pl.BlockSpec(memory_space=pl.ANY)
VECTOR = pl.BlockSpec(memory_space=pltpu.VMEM)


def call(kernel, name, shapes, in_specs, out_specs, scratch, products, limit):
    cost = pl.CostEstimate(
        flops=2 * products * 256**3, bytes_accessed=4 * 2**20, transcendentals=0
    )
    return pl.pallas_call(
        kernel,
        out_shape=shapes,
        in_specs=in_specs,
        out_specs=out_specs,
        scratch_shapes=scratch,
        compiler_params=pltpu.CompilerParams(vmem_limit_bytes=limit * 2**20),
        cost_estimate=cost,
        name=name,
    )


def pack(density):
    block = density.shape[2]
    sizes = (PART, MIDDLE, OUTER, WHOLE)
    shapes = [jax.ShapeDtypeStruct((1, size, block, block), density.dtype) for size in sizes]
    return call(pack_kernel, "pack", shapes, [VECTOR], [VECTOR] * len(sizes), [], 1, 8)(density)


def first(own, beside):
    block = own.shape[2]
    shape = jax.ShapeDtypeStruct((BAND, block, block), jnp.float32)
    return call(first_kernel, "first", shape, [VECTOR] * 2, VECTOR, [], 46, 16)(own, beside)


def bundle(*arrays):
    shape = list(arrays[0].shape)
    shape[1] = sum(array.shape[1] for array in arrays)
    shape = jax.ShapeDtypeStruct(tuple(shape), arrays[0].dtype)
    return call(bundle_kernel, "bundle", shape, [VECTOR] * len(arrays), VECTOR, [], 1, 4)(*arrays)


def cut(kernel, size, *arrays):
    shape = list(arrays[0].shape)
    shape[1] = size
    shape = jax.ShapeDtypeStruct(tuple(shape), arrays[0].dtype)
    return call(kernel, "cut", shape, [VECTOR] * len(arrays), VECTOR, [], 1, 4)(*arrays)


def second(own, sources, before):
    block = own.shape[2]
    shapes = [before, jax.ShapeDtypeStruct((4 * MIDDLE, block, block), own.dtype)]
    return call(
        second_kernel,
        "second",
        shapes,
        [VECTOR] + [ANYWHERE] * 4 + [VECTOR],
        [VECTOR] * 2,
        [pltpu.SemaphoreType.DMA((4,))],
        30,
        8,
    )(own, *sources, before)


def third(own, pure, other_pure, before):
    block = own.shape[2]
    shapes = [before, jax.ShapeDtypeStruct((1, block, block), own.dtype)]
    return call(third_kernel, "third", shapes, [VECTOR] * 4, [VECTOR] * 2, [], 30, 8)(
        own, pure, other_pure, before
    )


def last(keep, own, beside, middle, sources, outers, turned, before):
    block = own.shape[2]
    shape = jax.ShapeDtypeStruct((1, BAND, block, LANES), jnp.float32)
    return call(
        last_kernel,
        "last",
        shape,
        [SCALARS] + [VECTOR] * 13,
        ANYWHERE,
        [
            pltpu.VMEM((4 * (WHOLE + OUTER) + 2, block, block), own.dtype),
            pltpu.VMEM((BAND, block, block), own.dtype),
            pltpu.VMEM((BAND, block, LANES), jnp.float32),
            pltpu.VMEM((BAND, block, LANES), jnp.float32),
            pltpu.SemaphoreType.DMA((BAND,)),
        ],
        120,
        24,
    )(keep, own, beside, middle, *sources, *outers, turned, before)


def after(*arrays):
    return lax.optimization_barrier(arrays)


def body(density, pattern):
    axes = ("row", "col", "layer")
    rows = lax.axis_size(("row", "col"))
    layers = lax.axis_size("layer")
    width = density.shape[2] // layers

    def fetch(array, step):
        pairs = []
        for source in range(rows):
            for plane in range(layers):
                shift = 2 * step * (1 - 2 * (source % 2)) * (1 - 2 * (plane % 2))
                pairs.append((source * layers + plane, (source - shift) % rows * layers + plane))
        return lax.ppermute(array, axes, pairs)

    def fetch_diag(array):
        pairs = []
        for source in range(rows):
            shift = 2 if source // 2 % 2 else -2
            pairs.append((source, (source + shift) % rows))
        return lax.ppermute(array, ("row", "col"), pairs)

    def swap(array, axis, distance):
        peers = lax.axis_size(axis)
        return lax.ppermute(array, axis, [(peer, peer ^ distance) for peer in range(peers)])

    swap_cores = lambda array: swap(array, "col", 1)

    def swap_layers(array):
        peers = lax.axis_size("col")
        pairs = []
        for peer in range(peers):
            for plane in range(layers):
                pairs.append((peer * layers + plane, (peer ^ 1) * layers + (plane ^ 1)))
        return lax.ppermute(array, ("col", "layer"), pairs)

    beside = swap_cores(density)
    diag, middle, outer, pure = pack(density)
    diag = fetch_diag(diag)
    middle = fetch(middle, 2)
    outer = fetch(outer, 3)
    pure = swap(pure, "col", 2)
    sums = first(density, beside)
    sums, middle = after(sums, middle)
    far_middle = swap_layers(middle)
    far_diag = swap_layers(cut(swap_kernel, SENT, diag))
    late_outer = after(outer, far_middle)[0]
    far_outer = swap_layers(cut(rest_kernel, OUTER, diag, late_outer))
    near = bundle(middle, diag)
    other_near = swap_cores(near)
    ends = bundle(far_middle, outer, outer)
    other_ends = swap_cores(ends)
    sums, middle = second(density, [near, other_ends, other_near, far_middle], sums)
    far_outer, far_diag, pure = after(far_outer, far_diag, pure)
    other_pure = swap_cores(pure)
    sums, turned = third(density, pure, other_pure, sums)
    far = bundle(far_diag, far_outer)
    own_far = swap_cores(far)
    sources = [pure, near, own_far, other_pure, other_near, far]
    out = last(pattern, density, beside, middle, sources, (ends, other_ends), turned, sums)
    if width < LANES:
        layer = lax.axis_index("layer")
        out = lax.dynamic_slice_in_dim(out, layer * width % LANES, width, 3)
    return out


def solution(mesh):
    return jax.shard_map(
        body,
        mesh=mesh,
        in_specs=(P(("row", "col"), None, None, None), P(("row", "col"), None)),
        out_specs=P(("row", "col"), None, None, "layer"),
        check_vma=False,
    )
```

```python
import jax
import jax.numpy as jnp
from jax import lax
from jax.experimental import pallas as pl
from jax.experimental.pallas import tpu as pltpu
from jax.sharding import PartitionSpec as P

HALF = 6
BAND = 2 * HALF + 1
FORWARD = ((0, 1, 2, 3, 4, 5, -3, -5), (0, 1, 2, 3), (0, 1))
BACKWARD = ((0, 1, 2, 3, 4, -4, -5, -6), (0, 1, 2, -6), (0, 0))
SIZES = tuple(len(part) for part in FORWARD)
WHOLE, MIDDLE, OUTER = SIZES
LEFT_OUT = 6
PARTS = ((0, 1, 2), (3, 4, 5, 7))
PART = len(PARTS[1])
SENT = len(PARTS[0])
STARTS = (0, WHOLE, WHOLE + MIDDLE)
FETCHED = sum(SIZES)
LANES = 128
FRAME = range(-HALF, HALF + 1)


def places():
    held = {}
    for offset in FRAME:
        held[0, offset] = offset + HALF
    for offset in FRAME:
        held.setdefault((1, 1 + offset), BAND + offset + HALF)
    slot = 2 * BAND
    for other in (False, True):
        for parts, way in ((FORWARD, 1), (BACKWARD, -1)):
            for step, part in enumerate(parts):
                for offset in part:
                    row = way * 2 * (step + 1)
                    column = row + way * offset
                    if other:
                        row, column = 1 - row, 1 - column
                    if (row, column) not in held and (column, row) not in held:
                        held[row, column] = slot
                    slot += 1
    return held


HELD = places()
def stage(slot):
    if slot < 2 * BAND:
        return 0
    group, item = divmod(slot - 2 * BAND, FETCHED)
    if item < WHOLE:
        return 2 if group in (0, 3) else 3
    return 1 if item < WHOLE + MIDDLE else 4


def terms(column, stages=(0, 1, 2, 3, 4)):
    plain = {}
    turned = {}
    for row in FRAME:
        if abs(row - column) <= HALF:
            if (row, column) in HELD:
                slot, group = HELD[row, column], plain
            else:
                slot, group = HELD[column, row], turned
            if stage(slot) in stages:
                group[row] = slot
    return plain, turned


def pairs():
    def shared(one, two):
        return sum(len(first.keys() & other.keys()) for first, other in zip(terms(one), terms(two)))

    def best(left):
        if len(left) < 2:
            return 0, [left] if left else []
        choices = []
        for place in range(1, len(left)):
            count, rest = best(left[1:place] + left[place + 1 :])
            choices.append((count + shared(left[0], left[place]), [(left[0], left[place])] + rest))
        if len(left) % 2:
            count, rest = best(left[1:])
            choices.append((count, [(left[0],)] + rest))
        return max(choices, key=lambda choice: choice[0])

    return best(tuple(FRAME))[1]


PAIRS = pairs()


def product(lefts, blocks, turned):
    return lax.dot_general(
        jnp.concatenate(lefts, axis=1),
        jnp.concatenate(blocks, axis=1 if turned else 0),
        (((1,), (1 if turned else 0,)), ((), ())),
        preferred_element_type=jnp.float32,
    )


def column_product(left, block, column, stages):
    total = None
    for turned, group in enumerate(terms(column, stages)):
        if group:
            part = product(
                [left(row) for row in group], [block(slot) for slot in group.values()], turned
            )
            total = part if total is None else total + part
    return total


def part_products(left, part, columns):
    totals = [None] * len(columns)

    def add(place, value):
        totals[place] = value if totals[place] is None else totals[place] + value

    for turned in (0, 1):
        groups = [terms(column)[turned] for column in columns]
        both = [row for row in groups[0] if all(row in group for group in groups)]
        if len(columns) > 1 and both:
            blocks = [
                jnp.concatenate([part(group[row], turned) for group in groups], axis=0 if turned else 1)
                for row in both
            ]
            value = product([left(row) for row in both], blocks, turned)
            for place in range(len(columns)):
                add(place, value[:, place * LANES : (place + 1) * LANES])
        for place, group in enumerate(groups):
            alone = [row for row in group if len(columns) == 1 or row not in both]
            if alone:
                blocks = [part(group[row], turned) for row in alone]
                add(place, product([left(row) for row in alone], blocks, turned))
    return totals


def position():
    row = lax.axis_index(("row", "col"))
    return 1 - 2 * (row % 2), lax.axis_index("layer") % 2, (row + row // 2) % 2


def pack_kernel(density, diag, middle, outer, pure):
    way, layer_kind, row_kind = position()

    def bring(out, item, forward, backward, backwards):
        index = HALF + way * jnp.where(backwards == 0, forward, -backward)
        out[0, item] = density[0, index]

    for item in range(PART):
        one, other = PARTS[0][min(item, SENT - 1)], PARTS[1][item]
        forward = jnp.where(layer_kind == 0, FORWARD[0][one], FORWARD[0][other])
        backward = jnp.where(layer_kind == 0, BACKWARD[0][one], BACKWARD[0][other])
        bring(diag, item, forward, backward, row_kind)
    for out, step in ((middle, 1), (outer, 2)):
        for item in range(SIZES[step]):
            bring(out, item, FORWARD[step][item], BACKWARD[step][item], layer_kind)
    for item in range(WHOLE):
        bring(pure, item, FORWARD[0][item], BACKWARD[0][item], 1 - row_kind)


def frame_row(way, array):
    return lambda offset: array[0, HALF + way * offset]


def first_kernel(own, beside, sums):
    way, layer_kind, row_kind = position()
    left = frame_row(way, own)
    right = frame_row(way, beside)
    for column in FRAME:
        block = lambda slot: left(slot - HALF) if slot < BAND else right(slot - BAND - HALF)
        sums[column + HALF] = column_product(left, block, column, (0,))


def middle_place(slot):
    group, item = divmod(slot - 2 * BAND, FETCHED)
    return group * MIDDLE + item - WHOLE


def bundle_kernel(*refs):
    arrays, out = refs[:-1], refs[-1]
    place = 0
    for array in arrays:
        for item in range(array.shape[1]):
            out[0, place] = array[0, item]
            place += 1


def swap_kernel(diag, out):
    for item in range(SENT):
        out[0, item] = diag[0, item]


def rest_kernel(diag, outer, out):
    way, layer_kind, row_kind = position()

    @pl.when(layer_kind == 0)
    def _():
        for item in range(OUTER):
            out[0, item] = outer[0, item]

    @pl.when(layer_kind == 1)
    def _():
        out[0, 0] = diag[0, SENT]
        out[0, 1] = outer[0, 0]


def second_kernel(own, near, far, other_near, other_far, before, sums, held, sems):
    way, layer_kind, row_kind = position()
    copies = []
    for other, sources in enumerate(((near, far), (other_near, other_far))):
        for source, kind in zip(sources, (layer_kind, 1 - layer_kind)):
            copies.append(
                pltpu.make_async_copy(
                    source.at[0, pl.ds(0, MIDDLE)],
                    held.at[pl.ds((other * 2 + kind) * MIDDLE, MIDDLE)],
                    sems.at[len(copies)],
                )
            )
    for copy in copies:
        copy.start()
    for copy in copies:
        copy.wait()
    left = frame_row(way, own)
    for column in FRAME:
        block = lambda slot: held[middle_place(slot)]
        total = column_product(left, block, column, (1,))
        sums[column + HALF] = before[column + HALF] + (0.0 if total is None else total)


def third_kernel(own, pure, other_pure, before, sums, turned):
    way, layer_kind, row_kind = position()
    turned[0] = other_pure[0, LEFT_OUT].T
    left = frame_row(way, own)
    for kind in (0, 1):

        def block(slot):
            place, item = divmod(slot - 2 * BAND, FETCHED)
            return other_pure[0, item] if place >= 2 else pure[0, item]

        @pl.when(row_kind == kind)
        def _():
            for column in FRAME:
                total = column_product(left, block, column, (2 + kind,))
                sums[column + HALF] = before[column + HALF] + (0.0 if total is None else total)


def last_kernel(keep, own, beside, middle, *refs):
    sources, outers, refs = refs[:6], refs[6:8], refs[8:]
    turned, before, out, following, rounded, square, result, out_sems = refs
    way, layer_kind, row_kind = position()
    part = lax.axis_index("layer") * (own.shape[2] // lax.axis_size("layer")) // LANES

    def bring(source, first, size, target):
        for item in range(size):
            following[target + item] = source[0, first + item]

    for other in range(2):
        pure, near, far = sources[other * 3 : other * 3 + 3]
        kind = row_kind if other == 0 else 1 - row_kind
        bring(pure, 0, WHOLE, (other * 2 + kind) * WHOLE)
        base = (other * 2 + 1 - kind) * WHOLE
        last_item = base + PARTS[1][-1]
        ends = (4 * WHOLE + other * 2 * OUTER, 4 * WHOLE + (other * 2 + 1) * OUTER)
        even = layer_kind == 0
        spare = 4 * (WHOLE + OUTER) + other
        bring(near, MIDDLE, SENT, base + layer_kind * SENT)
        bring(far, 0, SENT, base + (1 - layer_kind) * SENT)
        following[jnp.where(even, spare, last_item)] = near[0, MIDDLE + SENT]
        for item in range(OUTER):
            following[jnp.where(even, *ends) + item] = outers[other][0, MIDDLE + item]
        following[jnp.where(even, last_item, ends[0])] = far[0, SENT]
        following[jnp.where(even, ends[1], ends[0] + 1)] = far[0, SENT + 1]
    following[(1 - row_kind) * WHOLE + LEFT_OUT] = turned[0]

    left = frame_row(way, own)

    def next_place(slot):
        group, item = divmod(slot - 2 * BAND, FETCHED)
        if item < WHOLE:
            return group * WHOLE + item
        return 4 * WHOLE + group * OUTER + item - WHOLE - MIDDLE

    for kind in (0, 1):

        @pl.when(row_kind == kind)
        def _():
            block = lambda slot: following[next_place(slot)]
            for column in FRAME:
                total = column_product(left, block, column, (3 - kind, 4))
                total = before[column + HALF] + (0.0 if total is None else total)
                total = total * keep[0, HALF + way * column].astype(jnp.float32)
                rounded[column + HALF] = total.astype(jnp.bfloat16)
                mine = total[:, :LANES]
                for piece in range(1, total.shape[1] // LANES):
                    lanes = slice(piece * LANES, (piece + 1) * LANES)
                    mine = jnp.where(part == piece, total[:, lanes], mine)
                square[column + HALF] = mine

    lanes = pl.ds(pl.multiple_of(part * LANES, LANES), LANES)

    def piece(slot, turned):
        if slot < BAND:
            array, index = own, (0, HALF + way * (slot - HALF))
        elif slot < 2 * BAND:
            array, index = beside, (0, HALF + way * (slot - BAND - HALF))
        elif stage(slot) == 1:
            array, index = middle, (middle_place(slot),)
        else:
            array, index = following, (next_place(slot),)
        return array[(*index, lanes, slice(None)) if turned else (*index, slice(None), lanes)]

    written = []
    for columns in PAIRS:
        totals = part_products(lambda row: rounded[row + HALF], piece, columns)
        for column, total in zip(columns, totals):
            total = total * keep[0, HALF + way * column].astype(jnp.float32)
            result[column + HALF] = 3.0 * square[column + HALF] - 2.0 * total
            copy = pltpu.make_async_copy(
                result.at[column + HALF], out.at[0, HALF + way * column], out_sems.at[column + HALF]
            )
            copy.start()
            written.append(copy)
    for copy in written:
        copy.wait()


SCALARS = pl.BlockSpec(memory_space=pltpu.SMEM)
ANYWHERE = pl.BlockSpec(memory_space=pl.ANY)
VECTOR = pl.BlockSpec(memory_space=pltpu.VMEM)


def call(kernel, name, shapes, in_specs, out_specs, scratch, products, limit):
    cost = pl.CostEstimate(
        flops=2 * products * 256**3, bytes_accessed=4 * 2**20, transcendentals=0
    )
    return pl.pallas_call(
        kernel,
        out_shape=shapes,
        in_specs=in_specs,
        out_specs=out_specs,
        scratch_shapes=scratch,
        compiler_params=pltpu.CompilerParams(vmem_limit_bytes=limit * 2**20),
        cost_estimate=cost,
        name=name,
    )


def pack(density):
    block = density.shape[2]
    sizes = (PART, MIDDLE, OUTER, WHOLE)
    shapes = [jax.ShapeDtypeStruct((1, size, block, block), density.dtype) for size in sizes]
    return call(pack_kernel, "pack", shapes, [VECTOR], [VECTOR] * len(sizes), [], 1, 8)(density)


def first(own, beside):
    block = own.shape[2]
    shape = jax.ShapeDtypeStruct((BAND, block, block), jnp.float32)
    return call(first_kernel, "first", shape, [VECTOR] * 2, VECTOR, [], 46, 16)(own, beside)


def bundle(*arrays):
    shape = list(arrays[0].shape)
    shape[1] = sum(array.shape[1] for array in arrays)
    shape = jax.ShapeDtypeStruct(tuple(shape), arrays[0].dtype)
    return call(bundle_kernel, "bundle", shape, [VECTOR] * len(arrays), VECTOR, [], 1, 4)(*arrays)


def cut(kernel, size, *arrays):
    shape = list(arrays[0].shape)
    shape[1] = size
    shape = jax.ShapeDtypeStruct(tuple(shape), arrays[0].dtype)
    return call(kernel, "cut", shape, [VECTOR] * len(arrays), VECTOR, [], 1, 4)(*arrays)


def second(own, sources, before):
    block = own.shape[2]
    shapes = [before, jax.ShapeDtypeStruct((4 * MIDDLE, block, block), own.dtype)]
    return call(
        second_kernel,
        "second",
        shapes,
        [VECTOR] + [ANYWHERE] * 4 + [VECTOR],
        [VECTOR] * 2,
        [pltpu.SemaphoreType.DMA((4,))],
        30,
        8,
    )(own, *sources, before)


def third(own, pure, other_pure, before):
    block = own.shape[2]
    shapes = [before, jax.ShapeDtypeStruct((1, block, block), own.dtype)]
    return call(third_kernel, "third", shapes, [VECTOR] * 4, [VECTOR] * 2, [], 30, 8)(
        own, pure, other_pure, before
    )


def last(keep, own, beside, middle, sources, outers, turned, before):
    block = own.shape[2]
    shape = jax.ShapeDtypeStruct((1, BAND, block, LANES), jnp.float32)
    return call(
        last_kernel,
        "last",
        shape,
        [SCALARS] + [VECTOR] * 13,
        ANYWHERE,
        [
            pltpu.VMEM((4 * (WHOLE + OUTER) + 2, block, block), own.dtype),
            pltpu.VMEM((BAND, block, block), own.dtype),
            pltpu.VMEM((BAND, block, LANES), jnp.float32),
            pltpu.VMEM((BAND, block, LANES), jnp.float32),
            pltpu.SemaphoreType.DMA((BAND,)),
        ],
        120,
        24,
    )(keep, own, beside, middle, *sources, *outers, turned, before)


def after(*arrays):
    return lax.optimization_barrier(arrays)


def body(density, pattern):
    axes = ("row", "col", "layer")
    rows = lax.axis_size(("row", "col"))
    layers = lax.axis_size("layer")
    width = density.shape[2] // layers

    def fetch(array, step):
        pairs = []
        for source in range(rows):
            for plane in range(layers):
                shift = 2 * step * (1 - 2 * (source % 2)) * (1 - 2 * (plane % 2))
                pairs.append((source * layers + plane, (source - shift) % rows * layers + plane))
        return lax.ppermute(array, axes, pairs)

    def fetch_diag(array):
        pairs = []
        for source in range(rows):
            shift = 2 if source // 2 % 2 else -2
            pairs.append((source, (source + shift) % rows))
        return lax.ppermute(array, ("row", "col"), pairs)

    def swap(array, axis, distance):
        peers = lax.axis_size(axis)
        return lax.ppermute(array, axis, [(peer, peer ^ distance) for peer in range(peers)])

    swap_cores = lambda array: swap(array, "col", 1)

    def swap_layers(array):
        peers = lax.axis_size("col")
        pairs = []
        for peer in range(peers):
            for plane in range(layers):
                pairs.append((peer * layers + plane, (peer ^ 1) * layers + (plane ^ 1)))
        return lax.ppermute(array, ("col", "layer"), pairs)

    beside = swap_cores(density)
    diag, middle, outer, pure = pack(density)
    diag = fetch_diag(diag)
    middle = fetch(middle, 2)
    outer = fetch(outer, 3)
    pure = swap(pure, "col", 2)
    sums = first(density, beside)
    far_middle = swap_layers(middle)
    far_diag = swap_layers(cut(swap_kernel, SENT, diag))
    late_outer = after(outer, far_middle)[0]
    far_outer = swap_layers(cut(rest_kernel, OUTER, diag, late_outer))
    near = bundle(middle, diag)
    other_near = swap_cores(near)
    ends = bundle(far_middle, outer, outer)
    other_ends = swap_cores(ends)
    sums, middle = second(density, [near, other_ends, other_near, far_middle], sums)
    far_outer, far_diag, pure = after(far_outer, far_diag, pure)
    other_pure = swap_cores(pure)
    sums, turned = third(density, pure, other_pure, sums)
    far = bundle(far_diag, far_outer)
    own_far = swap_cores(far)
    sources = [pure, near, own_far, other_pure, other_near, far]
    out = last(pattern, density, beside, middle, sources, (ends, other_ends), turned, sums)
    if width < LANES:
        layer = lax.axis_index("layer")
        out = lax.dynamic_slice_in_dim(out, layer * width % LANES, width, 3)
    return out


def solution(mesh):
    return jax.shard_map(
        body,
        mesh=mesh,
        in_specs=(P(("row", "col"), None, None, None), P(("row", "col"), None)),
        out_specs=P(("row", "col"), None, None, "layer"),
        check_vma=False,
    )
```

```python
import jax
import jax.numpy as jnp
from jax import lax
from jax.experimental import pallas as pl
from jax.experimental.pallas import tpu as pltpu
from jax.sharding import PartitionSpec as P

HALF = 6
BAND = 2 * HALF + 1
FORWARD = ((0, 1, 2, 3, 4, 5, -3, -5), (0, 1, 2, 3), (0, 1))
BACKWARD = ((0, 1, 2, 3, 4, -4, -5, -6), (0, 1, 2, -6), (0, 0))
SIZES = tuple(len(part) for part in FORWARD)
WHOLE, MIDDLE, OUTER = SIZES
LEFT_OUT = 6
PARTS = ((0, 1, 2), (3, 4, 5, 7))
PART = len(PARTS[1])
SENT = len(PARTS[0])
STARTS = (0, WHOLE, WHOLE + MIDDLE)
FETCHED = sum(SIZES)
LANES = 128
FRAME = range(-HALF, HALF + 1)


def places():
    held = {}
    for offset in FRAME:
        held[0, offset] = offset + HALF
    for offset in FRAME:
        held.setdefault((1, 1 + offset), BAND + offset + HALF)
    slot = 2 * BAND
    for other in (False, True):
        for parts, way in ((FORWARD, 1), (BACKWARD, -1)):
            for step, part in enumerate(parts):
                for offset in part:
                    row = way * 2 * (step + 1)
                    column = row + way * offset
                    if other:
                        row, column = 1 - row, 1 - column
                    if (row, column) not in held and (column, row) not in held:
                        held[row, column] = slot
                    slot += 1
    return held


HELD = places()
def stage(slot):
    if slot < 2 * BAND:
        return 0
    group, item = divmod(slot - 2 * BAND, FETCHED)
    if item < WHOLE:
        return 2 if group in (0, 3) else 3
    return 1 if item < WHOLE + MIDDLE else 4


def terms(column, stages=(0, 1, 2, 3, 4)):
    plain = {}
    turned = {}
    for row in FRAME:
        if abs(row - column) <= HALF:
            if (row, column) in HELD:
                slot, group = HELD[row, column], plain
            else:
                slot, group = HELD[column, row], turned
            if stage(slot) in stages:
                group[row] = slot
    return plain, turned


def pairs():
    def shared(one, two):
        return sum(len(first.keys() & other.keys()) for first, other in zip(terms(one), terms(two)))

    def best(left):
        if len(left) < 2:
            return 0, [left] if left else []
        choices = []
        for place in range(1, len(left)):
            count, rest = best(left[1:place] + left[place + 1 :])
            choices.append((count + shared(left[0], left[place]), [(left[0], left[place])] + rest))
        if len(left) % 2:
            count, rest = best(left[1:])
            choices.append((count, [(left[0],)] + rest))
        return max(choices, key=lambda choice: choice[0])

    return best(tuple(FRAME))[1]


PAIRS = pairs()


def product(lefts, blocks, turned):
    return lax.dot_general(
        jnp.concatenate(lefts, axis=1),
        jnp.concatenate(blocks, axis=1 if turned else 0),
        (((1,), (1 if turned else 0,)), ((), ())),
        preferred_element_type=jnp.float32,
    )


def column_product(left, block, column, stages):
    total = None
    for turned, group in enumerate(terms(column, stages)):
        if group:
            part = product(
                [left(row) for row in group], [block(slot) for slot in group.values()], turned
            )
            total = part if total is None else total + part
    return total


def part_products(left, part, columns):
    totals = [None] * len(columns)

    def add(place, value):
        totals[place] = value if totals[place] is None else totals[place] + value

    for turned in (0, 1):
        groups = [terms(column)[turned] for column in columns]
        both = [row for row in groups[0] if all(row in group for group in groups)]
        if len(columns) > 1 and both:
            blocks = [
                jnp.concatenate([part(group[row], turned) for group in groups], axis=0 if turned else 1)
                for row in both
            ]
            value = product([left(row) for row in both], blocks, turned)
            for place in range(len(columns)):
                add(place, value[:, place * LANES : (place + 1) * LANES])
        for place, group in enumerate(groups):
            alone = [row for row in group if len(columns) == 1 or row not in both]
            if alone:
                blocks = [part(group[row], turned) for row in alone]
                add(place, product([left(row) for row in alone], blocks, turned))
    return totals


def position():
    row = lax.axis_index(("row", "col"))
    return 1 - 2 * (row % 2), lax.axis_index("layer") % 2, (row + row // 2) % 2


def pack_kernel(density, diag, middle, outer, pure):
    way, layer_kind, row_kind = position()

    def bring(out, item, forward, backward, backwards):
        index = HALF + way * jnp.where(backwards == 0, forward, -backward)
        out[0, item] = density[0, index]

    for item in range(PART):
        one, other = PARTS[0][min(item, SENT - 1)], PARTS[1][item]
        forward = jnp.where(layer_kind == 0, FORWARD[0][one], FORWARD[0][other])
        backward = jnp.where(layer_kind == 0, BACKWARD[0][one], BACKWARD[0][other])
        bring(diag, item, forward, backward, row_kind)
    for out, step in ((middle, 1), (outer, 2)):
        for item in range(SIZES[step]):
            bring(out, item, FORWARD[step][item], BACKWARD[step][item], layer_kind)
    for item in range(WHOLE):
        bring(pure, item, FORWARD[0][item], BACKWARD[0][item], 1 - row_kind)


def frame_row(way, array):
    return lambda offset: array[0, HALF + way * offset]


def first_kernel(own, beside, sums):
    way, layer_kind, row_kind = position()
    left = frame_row(way, own)
    right = frame_row(way, beside)
    for column in FRAME:
        block = lambda slot: left(slot - HALF) if slot < BAND else right(slot - BAND - HALF)
        sums[column + HALF] = column_product(left, block, column, (0,))


def middle_place(slot):
    group, item = divmod(slot - 2 * BAND, FETCHED)
    return group * MIDDLE + item - WHOLE


def bundle_kernel(*refs):
    arrays, out = refs[:-1], refs[-1]
    place = 0
    for array in arrays:
        for item in range(array.shape[1]):
            out[0, place] = array[0, item]
            place += 1


def swap_kernel(diag, out):
    for item in range(SENT):
        out[0, item] = diag[0, item]


def rest_kernel(diag, outer, out):
    way, layer_kind, row_kind = position()

    @pl.when(layer_kind == 0)
    def _():
        for item in range(OUTER):
            out[0, item] = outer[0, item]

    @pl.when(layer_kind == 1)
    def _():
        out[0, 0] = diag[0, SENT]
        out[0, 1] = outer[0, 0]


def second_kernel(own, near, far, other_near, other_far, before, sums, held, sems):
    way, layer_kind, row_kind = position()
    copies = []
    for other, sources in enumerate(((near, far), (other_near, other_far))):
        for source, kind in zip(sources, (layer_kind, 1 - layer_kind)):
            copies.append(
                pltpu.make_async_copy(
                    source.at[0, pl.ds(0, MIDDLE)],
                    held.at[pl.ds((other * 2 + kind) * MIDDLE, MIDDLE)],
                    sems.at[len(copies)],
                )
            )
    for copy in copies:
        copy.start()
    for copy in copies:
        copy.wait()
    left = frame_row(way, own)
    for column in FRAME:
        block = lambda slot: held[middle_place(slot)]
        total = column_product(left, block, column, (1,))
        sums[column + HALF] = before[column + HALF] + (0.0 if total is None else total)


def third_kernel(own, pure, other_pure, before, sums, turned):
    way, layer_kind, row_kind = position()
    turned[0] = other_pure[0, LEFT_OUT].T
    left = frame_row(way, own)
    for kind in (0, 1):

        def block(slot):
            place, item = divmod(slot - 2 * BAND, FETCHED)
            return other_pure[0, item] if place >= 2 else pure[0, item]

        @pl.when(row_kind == kind)
        def _():
            for column in FRAME:
                total = column_product(left, block, column, (2 + kind,))
                sums[column + HALF] = before[column + HALF] + (0.0 if total is None else total)


def last_kernel(keep, own, beside, middle, *refs):
    sources, outers, refs = refs[:6], refs[6:8], refs[8:]
    turned, before, out, following, rounded, square, result, out_sems = refs
    way, layer_kind, row_kind = position()
    part = lax.axis_index("layer") * (own.shape[2] // lax.axis_size("layer")) // LANES

    def bring(source, first, size, target):
        for item in range(size):
            following[target + item] = source[0, first + item]

    for other in range(2):
        pure, near, far = sources[other * 3 : other * 3 + 3]
        kind = row_kind if other == 0 else 1 - row_kind
        bring(pure, 0, WHOLE, (other * 2 + kind) * WHOLE)
        base = (other * 2 + 1 - kind) * WHOLE
        last_item = base + PARTS[1][-1]
        ends = (4 * WHOLE + other * 2 * OUTER, 4 * WHOLE + (other * 2 + 1) * OUTER)
        even = layer_kind == 0
        spare = 4 * (WHOLE + OUTER) + other
        bring(near, MIDDLE, SENT, base + layer_kind * SENT)
        bring(far, 0, SENT, base + (1 - layer_kind) * SENT)
        following[jnp.where(even, spare, last_item)] = near[0, MIDDLE + SENT]
        for item in range(OUTER):
            following[jnp.where(even, *ends) + item] = outers[other][0, MIDDLE + item]
        following[jnp.where(even, last_item, ends[0])] = far[0, SENT]
        following[jnp.where(even, ends[1], ends[0] + 1)] = far[0, SENT + 1]
    following[(1 - row_kind) * WHOLE + LEFT_OUT] = turned[0]

    left = frame_row(way, own)

    def next_place(slot):
        group, item = divmod(slot - 2 * BAND, FETCHED)
        if item < WHOLE:
            return group * WHOLE + item
        return 4 * WHOLE + group * OUTER + item - WHOLE - MIDDLE

    for kind in (0, 1):

        @pl.when(row_kind == kind)
        def _():
            block = lambda slot: following[next_place(slot)]
            for column in FRAME:
                total = column_product(left, block, column, (3 - kind, 4))
                total = before[column + HALF] + (0.0 if total is None else total)
                total = total * keep[0, HALF + way * column].astype(jnp.float32)
                rounded[column + HALF] = total.astype(jnp.bfloat16)
                mine = total[:, :LANES]
                for piece in range(1, total.shape[1] // LANES):
                    lanes = slice(piece * LANES, (piece + 1) * LANES)
                    mine = jnp.where(part == piece, total[:, lanes], mine)
                square[column + HALF] = mine

    lanes = pl.ds(pl.multiple_of(part * LANES, LANES), LANES)

    def piece(slot, turned):
        if slot < BAND:
            array, index = own, (0, HALF + way * (slot - HALF))
        elif slot < 2 * BAND:
            array, index = beside, (0, HALF + way * (slot - BAND - HALF))
        elif stage(slot) == 1:
            array, index = middle, (middle_place(slot),)
        else:
            array, index = following, (next_place(slot),)
        return array[(*index, lanes, slice(None)) if turned else (*index, slice(None), lanes)]

    written = []
    for columns in PAIRS:
        totals = part_products(lambda row: rounded[row + HALF], piece, columns)
        for column, total in zip(columns, totals):
            total = total * keep[0, HALF + way * column].astype(jnp.float32)
            result[column + HALF] = 3.0 * square[column + HALF] - 2.0 * total
            copy = pltpu.make_async_copy(
                result.at[column + HALF], out.at[0, HALF + way * column], out_sems.at[column + HALF]
            )
            copy.start()
            written.append(copy)
    for copy in written:
        copy.wait()


SCALARS = pl.BlockSpec(memory_space=pltpu.SMEM)
ANYWHERE = pl.BlockSpec(memory_space=pl.ANY)
VECTOR = pl.BlockSpec(memory_space=pltpu.VMEM)


def call(kernel, name, shapes, in_specs, out_specs, scratch, products, limit):
    cost = pl.CostEstimate(
        flops=2 * products * 256**3, bytes_accessed=4 * 2**20, transcendentals=0
    )
    return pl.pallas_call(
        kernel,
        out_shape=shapes,
        in_specs=in_specs,
        out_specs=out_specs,
        scratch_shapes=scratch,
        compiler_params=pltpu.CompilerParams(vmem_limit_bytes=limit * 2**20),
        cost_estimate=cost,
        name=name,
    )


def pack(density):
    block = density.shape[2]
    sizes = (PART, MIDDLE, OUTER, WHOLE)
    shapes = [jax.ShapeDtypeStruct((1, size, block, block), density.dtype) for size in sizes]
    return call(pack_kernel, "pack", shapes, [VECTOR], [VECTOR] * len(sizes), [], 1, 8)(density)


def first(own, beside):
    block = own.shape[2]
    shape = jax.ShapeDtypeStruct((BAND, block, block), jnp.float32)
    return call(first_kernel, "first", shape, [VECTOR] * 2, VECTOR, [], 46, 16)(own, beside)


def bundle(*arrays):
    shape = list(arrays[0].shape)
    shape[1] = sum(array.shape[1] for array in arrays)
    shape = jax.ShapeDtypeStruct(tuple(shape), arrays[0].dtype)
    return call(bundle_kernel, "bundle", shape, [VECTOR] * len(arrays), VECTOR, [], 1, 4)(*arrays)


def cut(kernel, size, *arrays):
    shape = list(arrays[0].shape)
    shape[1] = size
    shape = jax.ShapeDtypeStruct(tuple(shape), arrays[0].dtype)
    return call(kernel, "cut", shape, [VECTOR] * len(arrays), VECTOR, [], 1, 4)(*arrays)


def second(own, sources, before):
    block = own.shape[2]
    shapes = [before, jax.ShapeDtypeStruct((4 * MIDDLE, block, block), own.dtype)]
    return call(
        second_kernel,
        "second",
        shapes,
        [VECTOR] + [ANYWHERE] * 4 + [VECTOR],
        [VECTOR] * 2,
        [pltpu.SemaphoreType.DMA((4,))],
        30,
        8,
    )(own, *sources, before)


def third(own, pure, other_pure, before):
    block = own.shape[2]
    shapes = [before, jax.ShapeDtypeStruct((1, block, block), own.dtype)]
    return call(third_kernel, "third", shapes, [VECTOR] * 4, [VECTOR] * 2, [], 30, 8)(
        own, pure, other_pure, before
    )


def last(keep, own, beside, middle, sources, outers, turned, before):
    block = own.shape[2]
    shape = jax.ShapeDtypeStruct((1, BAND, block, LANES), jnp.float32)
    return call(
        last_kernel,
        "last",
        shape,
        [SCALARS] + [VECTOR] * 13,
        ANYWHERE,
        [
            pltpu.VMEM((4 * (WHOLE + OUTER) + 2, block, block), own.dtype),
            pltpu.VMEM((BAND, block, block), own.dtype),
            pltpu.VMEM((BAND, block, LANES), jnp.float32),
            pltpu.VMEM((BAND, block, LANES), jnp.float32),
            pltpu.SemaphoreType.DMA((BAND,)),
        ],
        120,
        24,
    )(keep, own, beside, middle, *sources, *outers, turned, before)


def after(*arrays):
    return lax.optimization_barrier(arrays)


def body(density, pattern):
    axes = ("row", "col", "layer")
    rows = lax.axis_size(("row", "col"))
    layers = lax.axis_size("layer")
    width = density.shape[2] // layers

    def fetch(array, step):
        pairs = []
        for source in range(rows):
            for plane in range(layers):
                shift = 2 * step * (1 - 2 * (source % 2)) * (1 - 2 * (plane % 2))
                pairs.append((source * layers + plane, (source - shift) % rows * layers + plane))
        return lax.ppermute(array, axes, pairs)

    def fetch_diag(array):
        pairs = []
        for source in range(rows):
            shift = 2 if source // 2 % 2 else -2
            pairs.append((source, (source + shift) % rows))
        return lax.ppermute(array, ("row", "col"), pairs)

    def swap(array, axis, distance):
        peers = lax.axis_size(axis)
        return lax.ppermute(array, axis, [(peer, peer ^ distance) for peer in range(peers)])

    swap_cores = lambda array: swap(array, "col", 1)

    def swap_layers(array):
        peers = lax.axis_size("col")
        pairs = []
        for peer in range(peers):
            for plane in range(layers):
                pairs.append((peer * layers + plane, (peer ^ 1) * layers + (plane ^ 1)))
        return lax.ppermute(array, ("col", "layer"), pairs)

    beside = swap_cores(density)
    diag, middle, outer, pure = pack(density)
    diag = fetch_diag(diag)
    middle = fetch(middle, 2)
    pure = swap(pure, "col", 2)
    sums = first(density, beside)
    far_middle = swap_layers(middle)
    middle, outer = after(middle, outer)
    outer = fetch(outer, 3)
    far_diag = swap_layers(cut(swap_kernel, SENT, diag))
    late_outer = after(outer, far_middle)[0]
    far_outer = swap_layers(cut(rest_kernel, OUTER, diag, late_outer))
    near = bundle(middle, diag)
    other_near = swap_cores(near)
    ends = bundle(far_middle, outer, outer)
    other_ends = swap_cores(ends)
    sums, middle = second(density, [near, other_ends, other_near, far_middle], sums)
    far_outer, far_diag, pure = after(far_outer, far_diag, pure)
    other_pure = swap_cores(pure)
    sums, turned = third(density, pure, other_pure, sums)
    far = bundle(far_diag, far_outer)
    own_far = swap_cores(far)
    sources = [pure, near, own_far, other_pure, other_near, far]
    out = last(pattern, density, beside, middle, sources, (ends, other_ends), turned, sums)
    if width < LANES:
        layer = lax.axis_index("layer")
        out = lax.dynamic_slice_in_dim(out, layer * width % LANES, width, 3)
    return out


def solution(mesh):
    return jax.shard_map(
        body,
        mesh=mesh,
        in_specs=(P(("row", "col"), None, None, None), P(("row", "col"), None)),
        out_specs=P(("row", "col"), None, None, "layer"),
        check_vma=False,
    )
```
